32 devices in a mesh: dp: 4 (over y, x), expert: 8 (over z, core).
Axes of the slice: x: 2, y: 2, z: 4, core: 2. Of those that a mesh axis runs over, the one named last changes fastest.
Arguments:
- tokens: bfloat16 [4096, 2048], P(('dp', 'expert')), may hold values from -6 to 6
- tangent: bfloat16 [4096, 2048], P(('dp', 'expert')), may hold values from -16 to 16
- routes: int32 [4096, 4], P(('dp', 'expert')), may hold values from 0 to 7, all different within a row; in each aligned block of 128 rows (0 to 127, 128 to 255, ...) at most 72 rows name the same one
- gates: float32 [4096, 4], P(('dp', 'expert')), may hold values from 0.05 to 0.5
- w_gate: bfloat16 [8, 2048, 768], P('expert'), may hold values from -0.125 to 0.125
- w_up: bfloat16 [8, 2048, 768], P('expert'), may hold values from -0.125 to 0.125
- w_down: bfloat16 [8, 768, 2048], P('expert'), may hold values from -0.21875 to 0.21875
Outputs:
- product: float32 [4096, 2048], P(('dp', 'expert'))
The draws below stay inside these ranges and needn't reach their ends.
Inputs may be any that keep to these rules, and one draw needn't show every extreme that they name: `routes`: among the 512 pairs of the rows of one device, no expert is named more than 72 times, a bound that some block reaches.
All inputs are finite; a program needn't handle non-finite values.
Results may differ from the reference program's by a relative error of at most 0.005.
Values may be sent and summed in bfloat16 or wider, within the bound.
No kernel may reach another device: no remote copies, remote signals or barrier semaphores. Data moves between devices by JAX's collectives and lax.ppermute only.
A program may use at most 128 MiB of HBM per device.

```python
import math
import jax
import jax.numpy as jnp
import numpy as np
from jax import lax

D = 2048
FF = 768
TOP = 4
TOK_DEV = 128
EXPERTS = 8
CAP = 72
TOKENS = 4096
N_DP = 4
N_EXPERT = 8


def draw_tangent(key, part):
    position = jnp.arange(TOKENS, dtype=jnp.float32) / TOKENS
    rising = 1.0 + 2.0 * position
    values = jnp.clip(jax.random.normal(key, (TOKENS, D), jnp.float32), -4.0, 4.0)
    return (values * rising[:, None]).astype(jnp.bfloat16)


def block_levels(stream_key, extent, cuts, low, top_value):
    gain = 1.0
    for dim, parts in cuts:
        draws = jax.random.uniform(jax.random.fold_in(jax.random.fold_in(stream_key, 6), dim), (parts,), jnp.float32, low / len(cuts), top_value / len(cuts))
        gain = gain * jnp.repeat(jnp.exp(draws), extent[dim] // parts).reshape((-1,) + (1,) * (len(extent) - 1 - dim))
    return gain


def shared_out(rng, own, number, rows, number_of, top, limit, lean):
    sequence = jax.random.permutation(rng, number_of)
    crowded, common = shares(number_of, rows * top, limit, lean, True), shares(number_of, rows * top, limit, lean, False)
    places = jnp.arange(number_of)

    def named(sizes, offset_by):
        used = int((sizes > 0).sum())
        fixed = max(1, used // 4)
        moved = fixed + (places - fixed + offset_by * (used - fixed)) % max(1, number_of - fixed)
        return jnp.zeros((number_of,), jnp.int32).at[sequence[jnp.where(places < fixed, places, moved)]].set(jnp.asarray(sizes, jnp.int32))

    sizes = jnp.where(number % 4 == 0, named(crowded, number // 4), named(common, number - number // 4 - 1))
    mixed = jax.random.permutation(jax.random.fold_in(own, 3), number_of)
    donor, sink = mixed[0:number_of // 2 * 2:2], mixed[1:number_of // 2 * 2:2]
    slack = jnp.minimum(sizes[donor] - 1, limit - sizes[sink]) // 2
    slack = jnp.where((donor == sequence[0]) | (sink == sequence[0]) | (sizes[sink] == 0), 0, jnp.maximum(slack, 0))
    moved = jax.random.randint(jax.random.fold_in(own, 4), (number_of // 2,), 0, 1 << 20) % (slack + 1)
    sizes = sizes.at[donor].add(-moved).at[sink].add(moved)
    members = jnp.searchsorted(jnp.cumsum(sizes), jnp.arange(rows * top), side="right").astype(jnp.int32)
    table = members.reshape(top, rows).T
    table = table[jax.random.permutation(jax.random.fold_in(own, 1), rows)]
    offset_by = jax.random.randint(jax.random.fold_in(own, 2), (rows, 1), 0, top)
    return jnp.take_along_axis(table, (jnp.arange(top)[None, :] + offset_by) % top, axis=1)


def shares(amount, total, bound, lean, full):
    weights = [(1 << 20) // math.isqrt(standing ** lean) + 1 for standing in range(1, amount + 1)]
    largest = bound if full else min(bound, max(-(-total // amount), total * weights[0] // sum(weights)))
    least = 1 if total - largest >= amount - 1 else 0
    counts, surplus = [largest] + [least] * (amount - 1), total - largest - least * (amount - 1)
    while surplus > 0:
        candidates = [i for i in range(1, amount) if counts[i] < largest] or [i for i in range(1, amount) if counts[i] < bound]
        mass, left = sum([weights[i] for i in candidates]), surplus
        for i in candidates:
            addition = min(bound - counts[i], max(1, left * weights[i] // mass), surplus)
            counts[i] = counts[i] + addition
            surplus = surplus - addition
    return np.array(counts)


def scatter_about(own_key, dims, deviation, most, pieces=(), kind=jnp.bfloat16):
    gain = block_levels(own_key, dims, pieces, -0.22, 0.18) if pieces else 1.0
    array = jax.random.normal(own_key, dims, jnp.float32) * deviation * gain
    return jnp.minimum(jnp.maximum(array, -most), most).astype(kind)


def setup_inputs(seed: int = 0) -> dict:
    key_list = jax.random.split(jax.random.key(seed), 8)
    tokens = scatter_about(key_list[0], (TOKENS, D), 1.0, 6.0, ((0, 32),))
    tangent = draw_tangent(jax.random.fold_in(key_list[7], 71), 0)
    routes_keys = jax.random.split(jax.random.fold_in(key_list[2], 1), TOKENS // TOK_DEV)
    routes_turns = jax.random.permutation(jax.random.fold_in(key_list[2], 3), TOKENS // TOK_DEV)
    routes = jax.vmap(lambda own, number: shared_out(jax.random.fold_in(key_list[2], 2), own, number, TOK_DEV, EXPERTS, TOP, CAP, 2))(routes_keys, routes_turns).reshape((TOKENS, TOP))
    gates = jnp.clip(0.05 + 0.45 * jax.random.uniform(key_list[3], (TOKENS, TOP), jnp.float32) ** block_levels(key_list[3], (TOKENS, TOP), ((0, 32),), -0.2, 0.2), 0.05, 0.5)
    w_gate = scatter_about(key_list[4], (EXPERTS, D, FF), D ** -0.5, 0.125, ((0, 8),))
    w_up = scatter_about(key_list[5], (EXPERTS, D, FF), D ** -0.5, 0.125, ((0, 8),))
    w_down = scatter_about(key_list[6], (EXPERTS, FF, D), FF ** -0.5, 0.21875, ((0, 8),))
    return {"tokens": tokens, "tangent": tangent, "routes": routes, "gates": gates, "w_gate": w_gate, "w_up": w_up, "w_down": w_down}


def reference(tokens, tangent, routes, gates, w_gate, w_up, w_down):
    most_rows = CAP * N_DP * N_EXPERT
    flat_routes = routes.reshape(-1).astype(jnp.int32)
    flat_gates = gates.reshape(-1)
    pair_token = jnp.arange(TOKENS * TOP, dtype=jnp.int32) // TOP
    experts_iota = jnp.arange(EXPERTS, dtype=jnp.int32)

    def select(expert_id):
        chosen = flat_routes == expert_id
        index = jnp.nonzero(chosen, size=most_rows, fill_value=0)[0].astype(jnp.int32)
        number = jnp.sum(chosen.astype(jnp.int32))
        valid = jnp.arange(most_rows, dtype=jnp.int32) < number
        rows_tok = pair_token[index]
        gate_vals = jnp.where(valid, flat_gates[index], jnp.float32(0.0))
        return (rows_tok, gate_vals)

    def project(x_rows, gate_w, up_w):
        return (jnp.dot(x_rows, gate_w, preferred_element_type=jnp.float32), jnp.dot(x_rows, up_w, preferred_element_type=jnp.float32))

    def forward_step(carry, inputs):
        expert_id, gate_w, up_w, down_w = inputs
        rows_tok, gate_vals = select(expert_id)
        pre_a, pre_b = project(tokens[rows_tok], gate_w, up_w)
        tan_a, tan_b = project(tangent[rows_tok], gate_w, up_w)
        sigma = jax.nn.sigmoid(pre_a)
        act = pre_a * sigma
        slope = sigma * (1.0 + pre_a * (1.0 - sigma))
        hidden_tangent = (slope * tan_a * pre_b + act * tan_b).astype(jnp.bfloat16)
        pair_tangent = jnp.dot(hidden_tangent, down_w, preferred_element_type=jnp.float32).astype(jnp.bfloat16)
        carry = carry.at[rows_tok].add(gate_vals[:, None] * pair_tangent.astype(jnp.float32))
        return (carry, None)
    jv_vals, _ = lax.scan(forward_step, tangent.astype(jnp.float32), (experts_iota, w_gate, w_up, w_down))

    def backward_step(carry, inputs):
        expert_id, gate_w, up_w, down_w = inputs
        rows_tok, gate_vals = select(expert_id)
        pre_a, pre_b = project(tokens[rows_tok], gate_w, up_w)
        sigma = jax.nn.sigmoid(pre_a)
        act = pre_a * sigma
        slope = sigma * (1.0 + pre_a * (1.0 - sigma))
        pair_cotangent = (gate_vals[:, None] * jv_vals[rows_tok]).astype(jnp.bfloat16)
        back_vals = jnp.dot(pair_cotangent, down_w.T, preferred_element_type=jnp.float32)
        grad_gate = (back_vals * pre_b * slope).astype(jnp.bfloat16)
        grad_up = (back_vals * act).astype(jnp.bfloat16)
        pair_grad = (jnp.dot(grad_gate, gate_w.T, preferred_element_type=jnp.float32) + jnp.dot(grad_up, up_w.T, preferred_element_type=jnp.float32)).astype(jnp.bfloat16)
        carry = carry.at[rows_tok].add(pair_grad.astype(jnp.float32))
        return (carry, None)
    summed, _ = lax.scan(backward_step, jv_vals, (experts_iota, w_gate, w_up, w_down))
    curvature = jnp.sum(jv_vals * jv_vals)
    return summed * lax.rsqrt(curvature / (TOKENS * D) + 1e-06)
```

```python
import jax
import jax.numpy as jnp
from jax import lax
from jax.sharding import PartitionSpec as P

CONTRACT_LAST = (((1,), (1,)), ((), ()))


def dot(lhs, rhs):
    return jnp.dot(lhs, rhs, preferred_element_type=jnp.float32)


def dot_last(lhs, rhs):
    return lax.dot_general(lhs, rhs, CONTRACT_LAST, preferred_element_type=jnp.float32)


def both_cores(pairs):
    return [(2 * src + core, 2 * dst + core) for src, dst in pairs for core in range(2)]


def hop(rows, pairs):
    return lax.ppermute(rows, "expert", both_cores(pairs))


def line_gather(block, pos, count):
    going_right, going_left = {}, {}
    right = left = block
    for step in range(1, count):
        right_pairs = [(i, i + 1) for i in range(step - 1, count - 1)]
        left_pairs = [(i, i - 1) for i in range(1, count - step + 1)]
        if step - 1 > count - step:
            right = left = hop(jnp.where(pos >= step - 1, right, left), right_pairs + left_pairs)
        else:
            right, left = hop(right, right_pairs), hop(left, left_pairs)
        going_right[step], going_left[step] = right, left
    return [block] + [
        jnp.where(pos >= s, going_right[s], going_left[count - s]) for s in range(1, count)
    ]


def add_rows(own, came):
    return (own.astype(jnp.float32) + came.astype(jnp.float32)).astype(jnp.bfloat16)


def line_reduce(parts, pos, count):
    came_right = came_left = None
    for dist in range(count - 1, 0, -1):
        right, left = parts[count - dist], parts[dist]
        if came_right is not None:
            right, left = add_rows(right, came_right), add_rows(left, came_left)
        right_pairs = [(i, i + 1) for i in range(0, count - dist)]
        left_pairs = [(i, i - 1) for i in range(dist, count)]
        if count - dist < dist - 1:
            came_right = came_left = hop(
                jnp.where(pos <= count - 1 - dist, right, left), right_pairs + left_pairs
            )
        else:
            came_right, came_left = hop(right, right_pairs), hop(left, left_pairs)
    return (
        parts[0].astype(jnp.float32)
        + came_right.astype(jnp.float32)
        + came_left.astype(jnp.float32)
    )


def sum_everywhere(value, axis):
    size = lax.axis_size(axis)
    if size & (size - 1):
        return lax.psum(value, axis)
    step = 1
    while step < size:
        value = value + lax.ppermute(value, axis, [(i, i ^ step) for i in range(size)])
        step *= 2
    return value


def line_shards(tokens, tangent, routes, gates, w_gate, w_up, w_down):
    token_count, width = tokens.shape
    owners = lax.axis_size("expert")
    count = owners // 2
    me = lax.axis_index("expert")
    pos, core = me // 2, me % 2
    swap = [(i, i ^ 1) for i in range(owners)]

    gate_of = jnp.sum(
        jnp.where(
            routes[:, :, None] == jnp.arange(owners, dtype=jnp.int32)[None, None, :],
            gates[:, :, None],
            jnp.float32(0.0),
        ),
        axis=1,
    ).T
    gate_rows = jnp.stack(line_gather(gate_of, pos, count))
    own_gates = lax.dynamic_index_in_dim(gate_rows, me, 1, keepdims=False)
    sib_gates = lax.dynamic_index_in_dim(gate_rows, me ^ 1, 1, keepdims=False)

    weights = [(w_gate[0], w_up[0], w_down[0])]
    weights.append(tuple(lax.ppermute(w, "expert", swap) for w in weights[0]))

    halves = 2
    half = token_count // halves
    gathered = []
    after = None
    for h in range(halves):
        rows = slice(h * half, (h + 1) * half)
        both = jnp.concatenate([tokens[rows], tangent[rows]])
        if after is not None:
            both, _ = lax.optimization_barrier((both, after))
        slots = line_gather(both, pos, count)
        after = slots[-1]
        gathered.append(jnp.concatenate(slots))

    jv_home, kept = [], []
    for h in range(halves):
        rows = slice(h * half, (h + 1) * half)
        partial = None
        states = []
        for (gate_w, up_w, down_w), pair_gates in zip(weights, (own_gates, sib_gates)):
            g = pair_gates[:, rows].reshape(count * half, 1)
            pre = dot(gathered[h], gate_w).reshape(count, 2, half, -1)
            ups = dot(gathered[h], up_w).reshape(count, 2, half, -1)
            a, da = (pre[:, i].reshape(count * half, -1) for i in range(2))
            b, db = (ups[:, i].reshape(count * half, -1) for i in range(2))
            sigma = jax.nn.sigmoid(a)
            act = a * sigma
            slope = sigma * (1.0 + a * (1.0 - sigma))
            b_slope = b * slope
            hidden = (g * (b_slope * da + act * db)).astype(jnp.bfloat16)
            term = dot(hidden, down_w)
            partial = term if partial is None else partial + term
            states.append((g * b_slope, g * act))
        kept.append(states)
        parts = list(partial.astype(jnp.bfloat16).reshape(count, half, width))
        jv_home.append(tangent[rows].astype(jnp.float32) + line_reduce(parts, pos, count))

    summed = []
    for h in range(halves):
        jv_rows = jnp.concatenate(line_gather(jv_home[h].astype(jnp.bfloat16), pos, count))
        partial = None
        for (gate_w, up_w, down_w), (b_slope, act) in zip(weights, kept[h]):
            back = dot_last(jv_rows, down_w)
            grad_gate = (back * b_slope).astype(jnp.bfloat16)
            grad_up = (back * act).astype(jnp.bfloat16)
            term = dot_last(grad_gate, gate_w) + dot_last(grad_up, up_w)
            partial = term if partial is None else partial + term
        parts = list(partial.astype(jnp.bfloat16).reshape(count, half, width))
        summed.append(jv_home[h] + line_reduce(parts, pos, count))

    squares = sum(jnp.sum(jv * jv) for jv in jv_home)
    squares = jnp.full((8, 128), squares)
    squares = sum_everywhere(sum_everywhere(squares, "dp"), "expert")[0, 0]
    elements = token_count * width * lax.axis_size("dp") * owners
    scale = lax.rsqrt(squares / elements + 1e-06)
    return jnp.concatenate(summed) * scale


def owner_states(x_rows, gate_w, up_w):
    pre_a = dot(x_rows, gate_w)
    pre_b = dot(x_rows, up_w)
    sigma = jax.nn.sigmoid(pre_a)
    act = pre_a * sigma
    slope = sigma * (1.0 + pre_a * (1.0 - sigma))
    return (pre_b, act, slope)


def pair_shards(tokens, tangent, routes, gates, w_gate, w_up, w_down):
    token_count, model_width = tokens.shape
    top_k = routes.shape[1]
    owners = lax.axis_size("expert")
    expert_total = owners * w_gate.shape[0]
    capacity = pair_capacity(token_count, top_k, expert_total)
    slot_total = expert_total * capacity
    pair_count = token_count * top_k
    gate_w = w_gate[0]
    up_w = w_up[0]
    down_w = w_down[0]
    flat_routes = routes.reshape(pair_count)
    onehot = (flat_routes[:, None] == jnp.arange(expert_total, dtype=jnp.int32)[None, :]).astype(
        jnp.int32
    )
    before = jnp.cumsum(onehot, axis=0) - onehot
    slot_of = jnp.sum(before * onehot, axis=1)
    slot_index = flat_routes * capacity + slot_of
    slot_match = slot_index[None, :] == jnp.arange(slot_total, dtype=jnp.int32)[:, None]
    filled = jnp.any(slot_match, axis=1)
    pair_token = jnp.arange(pair_count, dtype=jnp.int32) // top_k
    source_token = jnp.sum(jnp.where(slot_match, pair_token[None, :], 0), axis=1)
    source_gate = jnp.sum(
        jnp.where(slot_match, gates.reshape(pair_count)[None, :], jnp.float32(0.0)), axis=1
    )
    keep_mask = filled.astype(jnp.bfloat16)[:, None]

    def exchange(rows):
        blocks = rows.reshape(owners, capacity, model_width)
        moved = lax.all_to_all(blocks, "expert", split_axis=0, concat_axis=0, tiled=True)
        return moved.reshape(slot_total, model_width)

    x_rows = exchange(jnp.take(tokens, source_token, axis=0) * keep_mask)
    v_rows = exchange(jnp.take(tangent, source_token, axis=0) * keep_mask)
    pre_b, act, slope = owner_states(x_rows, gate_w, up_w)
    tan_a = dot(v_rows, gate_w)
    tan_b = dot(v_rows, up_w)
    hidden_tangent = (slope * tan_a * pre_b + act * tan_b).astype(jnp.bfloat16)
    returned = exchange(dot(hidden_tangent, down_w).astype(jnp.bfloat16))
    picked_rows = jnp.take(returned, slot_index, axis=0)
    picked_rows = picked_rows.reshape(token_count, top_k, model_width)
    jv_vals = tangent.astype(jnp.float32) + jnp.sum(
        gates[:, :, None] * picked_rows.astype(jnp.float32), axis=1
    )
    cot_rows = exchange(
        (jnp.take(jv_vals, source_token, axis=0) * source_gate[:, None]).astype(jnp.bfloat16)
    )
    back_vals = dot_last(cot_rows, down_w)
    grad_gate = (back_vals * pre_b * slope).astype(jnp.bfloat16)
    grad_up = (back_vals * act).astype(jnp.bfloat16)
    pair_grad = dot_last(grad_gate, gate_w) + dot_last(grad_up, up_w)
    grad_rows = jnp.take(exchange(pair_grad.astype(jnp.bfloat16)), slot_index, axis=0)
    grad_rows = grad_rows.reshape(token_count, top_k, model_width)
    summed = jv_vals + jnp.sum(grad_rows.astype(jnp.float32), axis=1)
    global_sum = lax.psum(jnp.sum(jv_vals * jv_vals), ("dp", "expert"))
    element_count = token_count * lax.axis_size("dp") * owners * model_width
    return summed * lax.rsqrt(global_sum / element_count + 1e-06)


def pair_capacity(token_count, top_k, expert_total):
    return max(2, token_count * top_k * 9 // (8 * expert_total))


def shards(tokens, tangent, routes, gates, w_gate, w_up, w_down):
    token_count, top_k = routes.shape
    owners = lax.axis_size("expert")
    capacity = pair_capacity(token_count, top_k, owners * w_gate.shape[0])
    whole_blocks = owners % 2 == 0 and w_gate.shape[0] == 1 and token_count <= 2 * capacity
    form = line_shards if whole_blocks else pair_shards
    return form(tokens, tangent, routes, gates, w_gate, w_up, w_down)


def solution(mesh):
    placed = (
        P(("dp", "expert"), None),
        P(("dp", "expert"), None),
        P(("dp", "expert"), None),
        P(("dp", "expert"), None),
        P("expert", None, None),
        P("expert", None, None),
        P("expert", None, None),
    )
    return jax.shard_map(
        shards, mesh=mesh, in_specs=placed, out_specs=P(("dp", "expert"), None), check_vma=False
    )
```

```python
import functools

import jax
import jax.numpy as jnp
from jax import lax
from jax.experimental import pallas as pl
from jax.experimental.pallas import tpu as pltpu
from jax.sharding import PartitionSpec as P

CONTRACT_LAST = (((1,), (1,)), ((), ()))


def dot(lhs, rhs):
    return jnp.dot(lhs, rhs, preferred_element_type=jnp.float32)


def dot_last(lhs, rhs):
    return lax.dot_general(lhs, rhs, CONTRACT_LAST, preferred_element_type=jnp.float32)


CORES, SIDES, ENDS = 2, 2, 2
LINE = SIDES * ENDS
SIDE_PAIRS = ((0, 1), (1, 0), (2, 3), (3, 2))
INNER_PAIRS = ((1, 2), (2, 1))


def hop(rows, pairs):
    both_cores = [(CORES * a + core, CORES * b + core) for a, b in pairs for core in range(CORES)]
    return lax.ppermute(rows, "expert", both_cores)


def side_hop(rows):
    return hop(rows, SIDE_PAIRS)


def inner_hop(rows):
    return hop(rows, INNER_PAIRS)


def after(value, *earlier):
    return lax.optimization_barrier((value, earlier))[0]


def add_rows(own, came):
    return (own.astype(jnp.float32) + came.astype(jnp.float32)).astype(jnp.bfloat16)


def chunk_of(hidden):
    return 256 if hidden % 256 == 0 else hidden


def assemble(inner, parts, rows, out, first):
    own, side, near, near_end, far, far_end = parts
    out[pl.ds(first, rows), :] = own[...]
    out[pl.ds(first + rows, rows), :] = side[...]
    out[pl.ds(first + 2 * rows, rows), :] = jnp.where(inner, near[...], near_end[...])
    out[pl.ds(first + 3 * rows, rows), :] = jnp.where(inner, far[...], far_end[...])


def store_parts(total, rows, outs):
    for i, out in enumerate(outs):
        out[...] = total[pl.ds(i * rows, rows), :].astype(out.dtype)


def forward_kernel(chunks, inner_ref, *refs):
    x_parts, v_parts, refs = refs[:6], refs[6:12], refs[12:]
    g_ref, own_w, sib_w, refs = refs[0], refs[1:4], refs[4:7], refs[7:]
    outs, (b_out, a_out, xv, total) = refs[:LINE], refs[LINE:]
    rows = x_parts[0].shape[0]
    step = pl.program_id(0)

    @pl.when(step == 0)
    def _():
        inner = inner_ref[0] == 1
        assemble(inner, x_parts, rows, xv, 0)
        assemble(inner, v_parts, rows, xv, LINE * rows)
        total[...] = jnp.zeros_like(total)

    def work(weights):
        gate_w, up_w, down_w = weights
        pre = dot(xv[...], gate_w[0])
        ups = dot(xv[...], up_w[0])
        a, da = pre[: LINE * rows], pre[LINE * rows :]
        b, db = ups[: LINE * rows], ups[LINE * rows :]
        g = g_ref[0, :, :1]
        sigma = 1.0 / (1.0 + jnp.exp(-a))
        act = g * (a * sigma)
        b_slope = g * (sigma * (1.0 + a * (1.0 - sigma))) * b
        a_out[...] = act
        b_out[...] = b_slope
        hidden = (b_slope * da + act * db).astype(jnp.bfloat16)
        total[...] += dot(hidden, down_w[0])

    @pl.when(step < chunks)
    def _():
        work(own_w)

    @pl.when(step >= chunks)
    def _():
        work(sib_w)

    @pl.when(step == 2 * chunks - 1)
    def _():
        store_parts(total, rows, outs)


def backward_kernel(chunks, inner_ref, *refs):
    parts, (b_ref, a_ref), refs = refs[:6], refs[6:8], refs[8:]
    own_w, sib_w, refs = refs[:3], refs[3:6], refs[6:]
    outs, (jv, total) = refs[:LINE], refs[LINE:]
    rows = parts[0].shape[0]
    step = pl.program_id(0)

    @pl.when(step == 0)
    def _():
        assemble(inner_ref[0] == 1, parts, rows, jv, 0)
        total[...] = jnp.zeros_like(total)

    def work(weights):
        gate_w, up_w, down_w = weights
        back = dot_last(jv[...], down_w[0])
        grad_gate = (back * b_ref[...]).astype(jnp.bfloat16)
        grad_up = (back * a_ref[...]).astype(jnp.bfloat16)
        total[...] += dot_last(grad_gate, gate_w[0]) + dot_last(grad_up, up_w[0])

    @pl.when(step < chunks)
    def _():
        work(own_w)

    @pl.when(step >= chunks)
    def _():
        work(sib_w)

    @pl.when(step == 2 * chunks - 1)
    def _():
        store_parts(total, rows, outs)


def weight_specs(width, chunk, chunks):
    def own(step):
        return jnp.minimum(step, chunks - 1)

    def sib(step):
        return jnp.maximum(step - chunks, 0)

    specs = []
    for of in (own, sib):
        tall = pl.BlockSpec((1, width, chunk), lambda s, of=of: (0, 0, of(s)))
        wide = pl.BlockSpec((1, chunk, width), lambda s, of=of: (0, of(s), 0))
        specs += [tall, tall, wide]
    return specs


def kernel_call(kernel, name, inner, parts, states, weights, state_out):
    rows, width = parts[0].shape
    hidden = weights[0].shape[2]
    chunk = chunk_of(hidden)
    chunks = hidden // chunk
    line_rows = LINE * rows
    part_spec = pl.BlockSpec((rows, width), lambda s: (0, 0))
    state_spec = pl.BlockSpec((line_rows, chunk), lambda s: (0, s))
    part_outs = [jax.ShapeDtypeStruct((rows, width), jnp.float32)]
    part_outs += [jax.ShapeDtypeStruct((rows, width), jnp.bfloat16)] * (LINE - 1)
    state_outs = [jax.ShapeDtypeStruct((line_rows, 2 * hidden), jnp.float32)] * 2
    if state_out:
        state_specs = [pl.BlockSpec((1, line_rows, states[0].shape[2]), lambda s: (s // chunks, 0, 0))]
        out_specs, outs, dots, lines = [part_spec] * LINE + [state_spec] * 2, part_outs + state_outs, 5, 2
    else:
        state_specs = [state_spec] * 2
        out_specs, outs, dots, lines = [part_spec] * LINE, part_outs, 3, 1
    return pl.pallas_call(
        functools.partial(kernel, chunks),
        grid=(2 * chunks,),
        in_specs=[pl.BlockSpec(memory_space=pltpu.SMEM)]
        + [part_spec] * len(parts)
        + state_specs
        + weight_specs(width, chunk, chunks),
        out_specs=out_specs,
        out_shape=outs,
        scratch_shapes=[
            pltpu.VMEM((lines * line_rows, width), jnp.bfloat16),
            pltpu.VMEM((line_rows, width), jnp.float32),
        ],
        compiler_params=pltpu.CompilerParams(vmem_limit_bytes=40 * 2**20),
        cost_estimate=pl.CostEstimate(
            flops=2 * dots * line_rows * width * 2 * hidden,
            bytes_accessed=12 * hidden * width,
            transcendentals=0,
        ),
        name=name,
    )(inner, *parts, *states, *weights)


def sum_everywhere(value, axis):
    size = lax.axis_size(axis)
    if size & (size - 1):
        return lax.psum(value, axis)
    step = 1
    while step < size:
        value = value + lax.ppermute(value, axis, [(i, i ^ step) for i in range(size)])
        step *= 2
    return value


def line_shards(tokens, tangent, routes, gates, w_gate, w_up, w_down):
    token_count, width = tokens.shape
    owners = lax.axis_size("expert")
    me = lax.axis_index("expert")
    pos = me // CORES
    inner = (pos == 1) | (pos == 2)
    inner_flag = inner.astype(jnp.int32).reshape(1)
    half = token_count // 2

    own_weights = (w_gate, w_up, w_down)
    swap = [(i, i ^ 1) for i in range(owners)]
    weights = own_weights + tuple(lax.ppermute(w, "expert", swap) for w in own_weights)

    gate_of = jnp.sum(
        jnp.where(
            routes.T[:, None, :] == jnp.arange(owners, dtype=jnp.int32)[None, :, None],
            gates.T[:, None, :],
            jnp.float32(0.0),
        ),
        axis=0,
    )

    def pick(ends, inners):
        return jnp.where(inner, inners, ends)

    def gather(own):
        side, near = side_hop(own), inner_hop(own)
        near_end, far = side_hop(near), inner_hop(side)
        return (own, side, near, near_end, far, side_hop(far))

    xa, va = tokens[:half], tangent[:half]
    xa_parts, va_parts = gather(xa), gather(va)
    gate_parts = gather(gate_of)
    gate_rows = jnp.stack(
        [
            gate_parts[0],
            gate_parts[1],
            pick(gate_parts[3], gate_parts[2]),
            pick(gate_parts[5], gate_parts[4]),
        ]
    )
    pair_gates = [
        lax.dynamic_index_in_dim(gate_rows, expert, 1, keepdims=False) for expert in (me, me ^ 1)
    ]

    def gates_of(rows):
        columns = jnp.stack([g[:, rows].reshape(LINE * half, 1) for g in pair_gates])
        return jnp.broadcast_to(columns, (2, LINE * half, 128))

    def forward(x_parts, v_parts, rows):
        *parts, b_slope, act = kernel_call(
            forward_kernel, "forward", inner_flag, x_parts + v_parts, (gates_of(rows),), weights, True
        )
        return parts, (b_slope, act)

    def backward(jv_parts, states):
        return kernel_call(backward_kernel, "backward", inner_flag, jv_parts, states, weights, False)

    def home(parts, side, inner_last):
        return parts[0] + side.astype(jnp.float32) + pick(0.0, inner_last.astype(jnp.float32))

    xb, vb = after((tokens[half:], tangent[half:]), xa_parts[5], va_parts[5])
    xb_side, vb_side, xb_near, vb_near = side_hop(xb), side_hop(vb), inner_hop(xb), inner_hop(vb)
    pa, states_a = forward(xa_parts, va_parts, slice(0, half))
    came = side_hop(pick(pa[3], xb_near))
    xb_near_end, vb_near_end = came, side_hop(vb_near)
    xb_far, vb_far = inner_hop(xb_side), inner_hop(vb_side)
    sa_far = add_rows(pa[3], came)
    came = side_hop(pick(pa[2], xb_far))
    xb_far_end, vb_far_end = came, side_hop(vb_far)
    sa_side = inner_hop(sa_far)
    sa_near = add_rows(pa[2], came)
    came = side_hop(pick(pa[1], add_rows(pa[1], sa_side)))
    last = inner_hop(sa_near)
    pb, states_b = forward(
        (xb, xb_side, xb_near, xb_near_end, xb_far, xb_far_end),
        (vb, vb_side, vb_near, vb_near_end, vb_far, vb_far_end),
        slice(half, token_count),
    )
    jv_a = tangent[:half].astype(jnp.float32) + home(pa, came, last)

    def gather_and_reduce(own, parts):
        side, near = side_hop(own), inner_hop(own)
        came = side_hop(pick(parts[3], near))
        near_end, far = came, inner_hop(side)
        s_far = add_rows(parts[3], came)
        came = side_hop(pick(parts[2], far))
        far_end, s_side = came, inner_hop(s_far)
        s_near = add_rows(parts[2], came)
        came = side_hop(pick(parts[1], add_rows(parts[1], s_side)))
        last = inner_hop(s_near)
        return (own, side, near, near_end, far, far_end), home(parts, came, last)

    ja = jv_a.astype(jnp.bfloat16)
    ja_parts, sum_b = gather_and_reduce(ja, pb)
    ga = backward(ja_parts, states_a)
    jv_b = tangent[half:].astype(jnp.float32) + sum_b
    jb = jv_b.astype(jnp.bfloat16)
    jb_parts, grad_a = gather_and_reduce(jb, ga)

    squares = jnp.full((8, 128), jnp.sum(jv_a * jv_a) + jnp.sum(jv_b * jv_b))
    squares = sum_everywhere(sum_everywhere(squares, "dp"), "expert")

    gb = backward(jb_parts, states_b)
    came = side_hop(gb[3])
    s_far = add_rows(gb[3], came)
    came = side_hop(gb[2])
    s_side = inner_hop(s_far)
    s_near = add_rows(gb[2], came)
    q, _ = lax.optimization_barrier((pick(gb[1], add_rows(gb[1], s_side)), squares))
    came = side_hop(q)
    grad_b = home(gb, came, inner_hop(s_near))

    elements = token_count * width * lax.axis_size("dp") * owners
    scale = lax.rsqrt(squares[0, 0] / elements + 1e-06)
    return jnp.concatenate([(jv_a + grad_a) * scale, (jv_b + grad_b) * scale])


def owner_states(x_rows, gate_w, up_w):
    pre_a = dot(x_rows, gate_w)
    pre_b = dot(x_rows, up_w)
    sigma = jax.nn.sigmoid(pre_a)
    act = pre_a * sigma
    slope = sigma * (1.0 + pre_a * (1.0 - sigma))
    return (pre_b, act, slope)


def pair_shards(tokens, tangent, routes, gates, w_gate, w_up, w_down):
    token_count, model_width = tokens.shape
    top_k = routes.shape[1]
    owners = lax.axis_size("expert")
    expert_total = owners * w_gate.shape[0]
    capacity = pair_capacity(token_count, top_k, expert_total)
    slot_total = expert_total * capacity
    pair_count = token_count * top_k
    gate_w = w_gate[0]
    up_w = w_up[0]
    down_w = w_down[0]
    flat_routes = routes.reshape(pair_count)
    onehot = (flat_routes[:, None] == jnp.arange(expert_total, dtype=jnp.int32)[None, :]).astype(
        jnp.int32
    )
    before = jnp.cumsum(onehot, axis=0) - onehot
    slot_of = jnp.sum(before * onehot, axis=1)
    slot_index = flat_routes * capacity + slot_of
    slot_match = slot_index[None, :] == jnp.arange(slot_total, dtype=jnp.int32)[:, None]
    filled = jnp.any(slot_match, axis=1)
    pair_token = jnp.arange(pair_count, dtype=jnp.int32) // top_k
    source_token = jnp.sum(jnp.where(slot_match, pair_token[None, :], 0), axis=1)
    source_gate = jnp.sum(
        jnp.where(slot_match, gates.reshape(pair_count)[None, :], jnp.float32(0.0)), axis=1
    )
    keep_mask = filled.astype(jnp.bfloat16)[:, None]

    def exchange(rows):
        blocks = rows.reshape(owners, capacity, model_width)
        moved = lax.all_to_all(blocks, "expert", split_axis=0, concat_axis=0, tiled=True)
        return moved.reshape(slot_total, model_width)

    x_rows = exchange(jnp.take(tokens, source_token, axis=0) * keep_mask)
    v_rows = exchange(jnp.take(tangent, source_token, axis=0) * keep_mask)
    pre_b, act, slope = owner_states(x_rows, gate_w, up_w)
    tan_a = dot(v_rows, gate_w)
    tan_b = dot(v_rows, up_w)
    hidden_tangent = (slope * tan_a * pre_b + act * tan_b).astype(jnp.bfloat16)
    returned = exchange(dot(hidden_tangent, down_w).astype(jnp.bfloat16))
    picked_rows = jnp.take(returned, slot_index, axis=0)
    picked_rows = picked_rows.reshape(token_count, top_k, model_width)
    jv_vals = tangent.astype(jnp.float32) + jnp.sum(
        gates[:, :, None] * picked_rows.astype(jnp.float32), axis=1
    )
    cot_rows = exchange(
        (jnp.take(jv_vals, source_token, axis=0) * source_gate[:, None]).astype(jnp.bfloat16)
    )
    back_vals = dot_last(cot_rows, down_w)
    grad_gate = (back_vals * pre_b * slope).astype(jnp.bfloat16)
    grad_up = (back_vals * act).astype(jnp.bfloat16)
    pair_grad = dot_last(grad_gate, gate_w) + dot_last(grad_up, up_w)
    grad_rows = jnp.take(exchange(pair_grad.astype(jnp.bfloat16)), slot_index, axis=0)
    grad_rows = grad_rows.reshape(token_count, top_k, model_width)
    summed = jv_vals + jnp.sum(grad_rows.astype(jnp.float32), axis=1)
    global_sum = lax.psum(jnp.sum(jv_vals * jv_vals), ("dp", "expert"))
    element_count = token_count * lax.axis_size("dp") * owners * model_width
    return summed * lax.rsqrt(global_sum / element_count + 1e-06)


def pair_capacity(token_count, top_k, expert_total):
    return max(2, token_count * top_k * 9 // (8 * expert_total))


def shards(tokens, tangent, routes, gates, w_gate, w_up, w_down):
    token_count, top_k = routes.shape
    owners = lax.axis_size("expert")
    capacity = pair_capacity(token_count, top_k, owners * w_gate.shape[0])
    whole_blocks = (
        owners == CORES * LINE and w_gate.shape[0] == 1 and token_count <= CORES * capacity
    )
    form = line_shards if whole_blocks else pair_shards
    return form(tokens, tangent, routes, gates, w_gate, w_up, w_down)


def solution(mesh):
    placed = (
        P(("dp", "expert"), None),
        P(("dp", "expert"), None),
        P(("dp", "expert"), None),
        P(("dp", "expert"), None),
        P("expert", None, None),
        P("expert", None, None),
        P("expert", None, None),
    )
    return jax.shard_map(
        shards, mesh=mesh, in_specs=placed, out_specs=P(("dp", "expert"), None), check_vma=False
    )
```

```python
import functools

import jax
import jax.numpy as jnp
from jax import lax
from jax.experimental import pallas as pl
from jax.experimental.pallas import tpu as pltpu
from jax.sharding import PartitionSpec as P

CONTRACT_LAST = (((1,), (1,)), ((), ()))


def dot(lhs, rhs):
    return jnp.dot(lhs, rhs, preferred_element_type=jnp.float32)


def dot_last(lhs, rhs):
    return lax.dot_general(lhs, rhs, CONTRACT_LAST, preferred_element_type=jnp.float32)


CORES, SIDES, ENDS = 2, 2, 2
LINE = SIDES * ENDS
SIDE_PAIRS = ((0, 1), (1, 0), (2, 3), (3, 2))
INNER_PAIRS = ((1, 2), (2, 1))


def hop(rows, pairs):
    both_cores = [(CORES * a + core, CORES * b + core) for a, b in pairs for core in range(CORES)]
    return lax.ppermute(rows, "expert", both_cores)


def side_hop(rows):
    return hop(rows, SIDE_PAIRS)


def inner_hop(rows):
    return hop(rows, INNER_PAIRS)


def add_rows(own, came):
    return (own.astype(jnp.float32) + came.astype(jnp.float32)).astype(jnp.bfloat16)


def in_vmem(value):
    return pltpu.with_memory_space_constraint(value, pltpu.VMEM)


LANES = 128
GATE_PIECES = 3


def assemble(inner, parts, columns, out):
    own, side, near, near_end, far, far_end = parts
    rows = own.shape[0]
    out[pl.ds(0, rows), :] = own[:, columns]
    out[pl.ds(rows, rows), :] = side[:, columns]

    @pl.when(inner)
    def _():
        out[pl.ds(2 * rows, rows), :] = near[:, columns]
        out[pl.ds(3 * rows, rows), :] = far[:, columns]

    @pl.when(jnp.logical_not(inner))
    def _():
        out[pl.ds(2 * rows, rows), :] = near_end[:, columns]
        out[pl.ds(3 * rows, rows), :] = far_end[:, columns]


def store_parts(total, outs):
    for i, out in enumerate(outs):
        rows = out.shape[0]
        out[...] = total[pl.ds(i * rows, rows), :].astype(out.dtype)


def forward_kernel(owners, where_ref, *refs):
    parts, weights, outs, (b_out, a_out) = refs[:6], refs[6:12], refs[12:16], refs[16:18]
    x, v, gates, total = refs[18:]
    width, hidden = total.shape[1], weights[0].shape[2]
    inner = where_ref[0] == 1
    assemble(inner, parts, pl.ds(0, width), x)
    assemble(inner, parts, pl.ds(width, width), v)
    assemble(inner, parts, pl.ds(2 * width, LANES), gates)
    lane = lax.broadcasted_iota(jnp.int32, (1, LANES), 1)
    for i in range(CORES):
        gate_w, up_w, down_w = weights[3 * i : 3 * i + 3]
        expert = where_ref[1 + i]
        named = lane == expert
        for piece in range(1, GATE_PIECES):
            named = named | (lane == expert + piece * owners)
        g = jnp.sum(jnp.where(named, gates[...].astype(jnp.float32), 0.0), axis=1, keepdims=True)
        a, b = dot(x[...], gate_w[0]), dot(x[...], up_w[0])
        da, db = dot(v[...], gate_w[0]), dot(v[...], up_w[0])
        sigma = 1.0 / (1.0 + jnp.exp(-a))
        act = g * (a * sigma)
        b_slope = g * (sigma * (1.0 + a * (1.0 - sigma))) * b
        columns = pl.ds(i * hidden, hidden)
        a_out[:, columns] = act
        b_out[:, columns] = b_slope
        term = dot((b_slope * da + act * db).astype(jnp.bfloat16), down_w[0])
        if i == 0:
            total[...] = term
        else:
            total[...] += term
    store_parts(total, outs)


def backward_kernel(where_ref, *refs):
    parts, (b_ref, a_ref), weights, outs = refs[:6], refs[6:8], refs[8:14], refs[14:18]
    squares, jv, total = refs[18:]
    hidden = weights[0].shape[2]
    assemble(where_ref[0] == 1, parts, slice(None), jv)
    sums = jnp.zeros((1, LANES), jnp.float32)
    for start in range(0, jv.shape[1], LANES):
        piece = jv[:, pl.ds(start, LANES)].astype(jnp.float32)
        sums = sums + jnp.sum(piece * piece, axis=0, keepdims=True)
    squares[...] = jnp.broadcast_to(sums, squares.shape)
    for i in range(CORES):
        gate_w, up_w, down_w = weights[3 * i : 3 * i + 3]
        columns = pl.ds(i * hidden, hidden)
        back = dot_last(jv[...], down_w[0])
        grad_gate = (back * b_ref[:, columns]).astype(jnp.bfloat16)
        grad_up = (back * a_ref[:, columns]).astype(jnp.bfloat16)
        term = dot_last(grad_gate, gate_w[0]) + dot_last(grad_up, up_w[0])
        if i == 0:
            total[...] = term
        else:
            total[...] += term
    store_parts(total, outs)


def kernel_call(kernel, name, where, operands, rows, width, extra_outs, scratch, flops):
    vmem = pl.BlockSpec(memory_space=pltpu.VMEM)
    outs = [pltpu.VMEM((rows, width), jnp.float32)]
    outs += [pltpu.VMEM((rows, width), jnp.bfloat16)] * (LINE - 1) + extra_outs
    return pl.pallas_call(
        kernel,
        in_specs=[pl.BlockSpec(memory_space=pltpu.SMEM)] + [vmem] * len(operands),
        out_specs=[vmem] * len(outs),
        out_shape=outs,
        scratch_shapes=scratch + [pltpu.VMEM((LINE * rows, width), jnp.float32)],
        compiler_params=pltpu.CompilerParams(vmem_limit_bytes=24 * 2**20),
        cost_estimate=pl.CostEstimate(flops=flops, bytes_accessed=0, transcendentals=0),
        name=name,
    )(where, *[in_vmem(value) for value in operands])


def exchange_sum(value, axis, step):
    pairs = [(i, i ^ step) for i in range(lax.axis_size(axis))]
    return value + lax.ppermute(value, axis, pairs)


def gate_pieces(routes, gates, owners):
    rest = jnp.sum(
        jnp.where(
            routes[:, :, None] == jnp.arange(owners, dtype=jnp.int32)[None, None, :],
            gates[:, :, None],
            jnp.float32(0.0),
        ),
        axis=1,
    )
    pieces = []
    for _ in range(GATE_PIECES):
        piece = lax.reduce_precision(rest, 8, 7)
        pieces.append(piece.astype(jnp.bfloat16))
        rest = rest - piece
    return jnp.pad(jnp.concatenate(pieces, axis=1), ((0, 0), (0, LANES - GATE_PIECES * owners)))


def line_shards(tokens, tangent, routes, gates, w_gate, w_up, w_down):
    token_count, width = tokens.shape
    hidden = w_gate.shape[2]
    owners = lax.axis_size("expert")
    me = lax.axis_index("expert")
    pos = me // CORES
    inner = (pos == 1) | (pos == 2)
    where = jnp.stack([inner.astype(jnp.int32), me, me ^ 1])
    half = token_count // 2
    line_rows = LINE * half
    swap = [(i, i ^ 1) for i in range(owners)]

    def pick(ends, inners):
        return jnp.where(inner, inners, ends)

    def home(parts, side, inner_last):
        return parts[0] + side.astype(jnp.float32) + pick(0.0, inner_last.astype(jnp.float32))

    def forward(parts):
        state = pltpu.VMEM((line_rows, CORES * hidden), jnp.float32)
        rows = pltpu.VMEM((line_rows, width), jnp.bfloat16)
        *outs, b_slope, act = kernel_call(
            functools.partial(forward_kernel, owners),
            "forward",
            where,
            (*parts, *weights),
            half,
            width,
            [state, state],
            [rows, rows, pltpu.VMEM((line_rows, LANES), jnp.bfloat16)],
            2 * 5 * line_rows * width * CORES * hidden,
        )
        return outs, (b_slope, act)

    def backward(parts, states):
        *outs, squares = kernel_call(
            backward_kernel,
            "backward",
            where,
            (*parts, *states, *weights),
            half,
            width,
            [pltpu.VMEM((8, LANES), jnp.float32)],
            [pltpu.VMEM((line_rows, width), jnp.bfloat16)],
            2 * 3 * line_rows * width * CORES * hidden,
        )
        return outs, squares

    pieces = gate_pieces(routes, gates, owners)
    halves = [slice(0, half), slice(half, token_count)]
    load_a, load_b = (
        jnp.concatenate([tokens[rows], tangent[rows], pieces[rows]], axis=1) for rows in halves
    )

    def slot(*results):
        return lax.optimization_barrier(results)

    def both_ways(part, payload):
        first = pick(part, payload[:, :width])
        if payload.shape[1] > width:
            first = jnp.concatenate([first, payload[:, width:]], axis=1)
        return side_hop(first)

    a_side, a_near, sib_gate, w_up, w_down, load_b = slot(
        side_hop(load_a), inner_hop(load_a), lax.ppermute(w_gate, "expert", swap), w_up, w_down, load_b
    )
    a_near_end, a_far, sib_up, w_down, load_b = slot(
        side_hop(a_near), inner_hop(a_side), lax.ppermute(w_up, "expert", swap), w_down, load_b
    )
    a_far_end, sib_down, load_b = slot(side_hop(a_far), lax.ppermute(w_down, "expert", swap), load_b)
    weights = (w_gate, w_up, w_down, sib_gate, sib_up, sib_down)

    b_side, b_near, (pa, states_a) = slot(
        side_hop(load_b),
        inner_hop(load_b),
        forward((load_a, a_side, a_near, a_near_end, a_far, a_far_end)),
    )
    b_near_end, b_far = slot(both_ways(pa[3], b_near), inner_hop(b_side))
    sa_far = add_rows(pa[3], b_near_end[:, :width])
    b_far_end, sa_side = slot(both_ways(pa[2], b_far), inner_hop(sa_far))
    sa_near = add_rows(pa[2], b_far_end[:, :width])
    came, last, (pb, states_b) = slot(
        both_ways(pa[1], add_rows(pa[1], sa_side)),
        inner_hop(sa_near),
        forward((load_b, b_side, b_near, b_near_end, b_far, b_far_end)),
    )
    jv_a = tangent[:half].astype(jnp.float32) + home(pa, came, last)

    def gather_and_reduce(own, parts, work):
        side, near = slot(side_hop(own), inner_hop(own))
        near_end, far = slot(both_ways(parts[3], near), inner_hop(side))
        s_far = add_rows(parts[3], near_end)
        far_end, s_side = slot(both_ways(parts[2], far), inner_hop(s_far))
        s_near = add_rows(parts[2], far_end)
        came, last, worked = slot(
            both_ways(parts[1], add_rows(parts[1], s_side)),
            inner_hop(s_near),
            work((own, side, near, near_end, far, far_end)),
        )
        return worked, home(parts, came, last)

    (ga, squares_a), sum_b = gather_and_reduce(
        jv_a.astype(jnp.bfloat16), pb, lambda parts: backward(parts, states_a)
    )
    jv_b = tangent[half:].astype(jnp.float32) + sum_b
    (gb, squares_b), grad_a = gather_and_reduce(
        jv_b.astype(jnp.bfloat16), ga, lambda parts: backward(parts, states_b)
    )

    sum_a = jv_a + grad_a
    lines = lax.axis_size("dp")
    first, second = side_hop(gb[3]), side_hop(gb[2])
    first, squares = slot(first, exchange_sum(squares_a + squares_b, "expert", 1))
    step = 1
    while step < lines // 2:
        squares = exchange_sum(squares, "dp", step)
        step *= 2
    s_near = add_rows(gb[2], second)
    s_side, second, squares = slot(inner_hop(add_rows(gb[3], first)), second, squares)
    came, last = side_hop(pick(gb[1], add_rows(gb[1], s_side))), inner_hop(s_near)
    while step < lines:
        squares = exchange_sum(squares, "dp", step)
        step *= 2
    grad_b = home(gb, came, last)

    elements = token_count * width * lax.axis_size("dp") * owners
    scale = lax.rsqrt(jnp.sum(squares[0]) / elements + 1e-06)
    return jnp.concatenate([sum_a * scale, (jv_b + grad_b) * scale])


def owner_states(x_rows, gate_w, up_w):
    pre_a = dot(x_rows, gate_w)
    pre_b = dot(x_rows, up_w)
    sigma = jax.nn.sigmoid(pre_a)
    act = pre_a * sigma
    slope = sigma * (1.0 + pre_a * (1.0 - sigma))
    return (pre_b, act, slope)


def pair_shards(tokens, tangent, routes, gates, w_gate, w_up, w_down):
    token_count, model_width = tokens.shape
    top_k = routes.shape[1]
    owners = lax.axis_size("expert")
    expert_total = owners * w_gate.shape[0]
    capacity = pair_capacity(token_count, top_k, expert_total)
    slot_total = expert_total * capacity
    pair_count = token_count * top_k
    gate_w = w_gate[0]
    up_w = w_up[0]
    down_w = w_down[0]
    flat_routes = routes.reshape(pair_count)
    onehot = (flat_routes[:, None] == jnp.arange(expert_total, dtype=jnp.int32)[None, :]).astype(
        jnp.int32
    )
    before = jnp.cumsum(onehot, axis=0) - onehot
    slot_of = jnp.sum(before * onehot, axis=1)
    slot_index = flat_routes * capacity + slot_of
    slot_match = slot_index[None, :] == jnp.arange(slot_total, dtype=jnp.int32)[:, None]
    filled = jnp.any(slot_match, axis=1)
    pair_token = jnp.arange(pair_count, dtype=jnp.int32) // top_k
    source_token = jnp.sum(jnp.where(slot_match, pair_token[None, :], 0), axis=1)
    source_gate = jnp.sum(
        jnp.where(slot_match, gates.reshape(pair_count)[None, :], jnp.float32(0.0)), axis=1
    )
    keep_mask = filled.astype(jnp.bfloat16)[:, None]

    def exchange(rows):
        blocks = rows.reshape(owners, capacity, model_width)
        moved = lax.all_to_all(blocks, "expert", split_axis=0, concat_axis=0, tiled=True)
        return moved.reshape(slot_total, model_width)

    x_rows = exchange(jnp.take(tokens, source_token, axis=0) * keep_mask)
    v_rows = exchange(jnp.take(tangent, source_token, axis=0) * keep_mask)
    pre_b, act, slope = owner_states(x_rows, gate_w, up_w)
    tan_a = dot(v_rows, gate_w)
    tan_b = dot(v_rows, up_w)
    hidden_tangent = (slope * tan_a * pre_b + act * tan_b).astype(jnp.bfloat16)
    returned = exchange(dot(hidden_tangent, down_w).astype(jnp.bfloat16))
    picked_rows = jnp.take(returned, slot_index, axis=0)
    picked_rows = picked_rows.reshape(token_count, top_k, model_width)
    jv_vals = tangent.astype(jnp.float32) + jnp.sum(
        gates[:, :, None] * picked_rows.astype(jnp.float32), axis=1
    )
    cot_rows = exchange(
        (jnp.take(jv_vals, source_token, axis=0) * source_gate[:, None]).astype(jnp.bfloat16)
    )
    back_vals = dot_last(cot_rows, down_w)
    grad_gate = (back_vals * pre_b * slope).astype(jnp.bfloat16)
    grad_up = (back_vals * act).astype(jnp.bfloat16)
    pair_grad = dot_last(grad_gate, gate_w) + dot_last(grad_up, up_w)
    grad_rows = jnp.take(exchange(pair_grad.astype(jnp.bfloat16)), slot_index, axis=0)
    grad_rows = grad_rows.reshape(token_count, top_k, model_width)
    summed = jv_vals + jnp.sum(grad_rows.astype(jnp.float32), axis=1)
    global_sum = lax.psum(jnp.sum(jv_vals * jv_vals), ("dp", "expert"))
    element_count = token_count * lax.axis_size("dp") * owners * model_width
    return summed * lax.rsqrt(global_sum / element_count + 1e-06)


def pair_capacity(token_count, top_k, expert_total):
    return max(2, token_count * top_k * 9 // (8 * expert_total))


def shards(tokens, tangent, routes, gates, w_gate, w_up, w_down):
    token_count, top_k = routes.shape
    owners = lax.axis_size("expert")
    capacity = pair_capacity(token_count, top_k, owners * w_gate.shape[0])
    dp = lax.axis_size("dp")
    whole_blocks = (
        owners == CORES * LINE
        and dp & (dp - 1) == 0
        and w_gate.shape[0] == 1
        and token_count <= CORES * capacity
    )
    form = line_shards if whole_blocks else pair_shards
    return form(tokens, tangent, routes, gates, w_gate, w_up, w_down)


def solution(mesh):
    placed = (
        P(("dp", "expert"), None),
        P(("dp", "expert"), None),
        P(("dp", "expert"), None),
        P(("dp", "expert"), None),
        P("expert", None, None),
        P("expert", None, None),
        P("expert", None, None),
    )
    return jax.shard_map(
        shards, mesh=mesh, in_specs=placed, out_specs=P(("dp", "expert"), None), check_vma=False
    )
```

```python
import functools

import jax
import jax.numpy as jnp
from jax import lax
from jax.experimental import pallas as pl
from jax.experimental.pallas import tpu as pltpu
from jax.sharding import PartitionSpec as P

CONTRACT_LAST = (((1,), (1,)), ((), ()))


def dot(lhs, rhs):
    return jnp.dot(lhs, rhs, preferred_element_type=jnp.float32)


def dot_last(lhs, rhs):
    return lax.dot_general(lhs, rhs, CONTRACT_LAST, preferred_element_type=jnp.float32)


CORES, SIDES, ENDS = 2, 2, 2
LINE = SIDES * ENDS
SIDE_PAIRS = ((0, 1), (1, 0), (2, 3), (3, 2))
INNER_PAIRS = ((1, 2), (2, 1))


END_CHIPS = (0, 3)


def both_cores(pairs):
    return [(CORES * a + core, CORES * b + core) for a, b in pairs for core in range(CORES)]


def side_hop(rows):
    return lax.ppermute(rows, "expert", both_cores(SIDE_PAIRS))


def inner_hop(rows):
    idle = [(CORES * a + core, CORES * a + 1 - core) for a in END_CHIPS for core in range(CORES)]
    return lax.ppermute(rows, "expert", both_cores(INNER_PAIRS) + idle)


def add_rows(own, came):
    return (own.astype(jnp.float32) + came.astype(jnp.float32)).astype(jnp.bfloat16)


def in_vmem(value):
    return pltpu.with_memory_space_constraint(value, pltpu.VMEM)


LANES = 128
GATE_PIECES = 3


def fetch(inner, parts, out, sems):
    own, side, near, near_end, far, far_end = parts
    rows = own.shape[0]

    def copies(blocks, first):
        return [
            pltpu.make_async_copy(block, out.at[pl.ds(i * rows, rows), :], sems.at[i])
            for i, block in enumerate(blocks, first)
        ]

    def begin(blocks, first):
        for copy in copies(blocks, first):
            copy.start()

    def finish(blocks, first):
        for copy in copies(blocks, first):
            copy.wait()

    for act in (begin, finish):
        act((own, side), 0)
        pl.when(inner)(functools.partial(act, (near, far), 2))
        pl.when(jnp.logical_not(inner))(functools.partial(act, (near_end, far_end), 2))


def store_parts(total, outs):
    for i, out in enumerate(outs):
        rows = out.shape[0]
        out[...] = total[pl.ds(i * rows, rows), :].astype(out.dtype)


def forward_kernel(owners, where_ref, *refs):
    parts, weights, outs, (b_out, a_out) = refs[:6], refs[6:12], refs[12:16], refs[16:18]
    sems, load, total = refs[18:]
    width, hidden = total.shape[1], weights[0].shape[2]
    fetch(where_ref[0] == 1, parts, load, sems)
    x, v = load.at[:, pl.ds(0, width)], load.at[:, pl.ds(width, width)]
    gates = load.at[:, pl.ds(2 * width, LANES)]
    lane = lax.broadcasted_iota(jnp.int32, (1, LANES), 1)
    for i in range(CORES):
        gate_w, up_w, down_w = weights[3 * i : 3 * i + 3]
        expert = where_ref[1 + i]
        named = lane == expert
        for piece in range(1, GATE_PIECES):
            named = named | (lane == expert + piece * owners)
        g = jnp.sum(jnp.where(named, gates[...].astype(jnp.float32), 0.0), axis=1, keepdims=True)
        a, b = dot(x[...], gate_w[0]), dot(x[...], up_w[0])
        da, db = dot(v[...], gate_w[0]), dot(v[...], up_w[0])
        sigma = 1.0 / (1.0 + jnp.exp(-a))
        act = g * (a * sigma)
        b_slope = g * (sigma * (1.0 + a * (1.0 - sigma))) * b
        columns = pl.ds(i * hidden, hidden)
        a_out[:, columns] = act
        b_out[:, columns] = b_slope
        term = dot((b_slope * da + act * db).astype(jnp.bfloat16), down_w[0])
        if i == 0:
            total[...] = term
        else:
            total[...] += term
    store_parts(total, outs)


def backward_kernel(where_ref, *refs):
    parts, (b_ref, a_ref), weights, outs = refs[:6], refs[6:8], refs[8:14], refs[14:18]
    squares, sems, jv, total = refs[18:]
    hidden = weights[0].shape[2]
    fetch(where_ref[0] == 1, parts, jv, sems)
    sums = jnp.zeros((1, LANES), jnp.float32)
    for start in range(0, jv.shape[1], LANES):
        piece = jv[:, pl.ds(start, LANES)].astype(jnp.float32)
        sums = sums + jnp.sum(piece * piece, axis=0, keepdims=True)
    squares[...] = jnp.broadcast_to(sums, squares.shape)
    for i in range(CORES):
        gate_w, up_w, down_w = weights[3 * i : 3 * i + 3]
        columns = pl.ds(i * hidden, hidden)
        back = dot_last(jv[...], down_w[0])
        grad_gate = (back * b_ref[:, columns]).astype(jnp.bfloat16)
        grad_up = (back * a_ref[:, columns]).astype(jnp.bfloat16)
        term = dot_last(grad_gate, gate_w[0]) + dot_last(grad_up, up_w[0])
        if i == 0:
            total[...] = term
        else:
            total[...] += term
    store_parts(total, outs)


def kernel_call(kernel, name, where, parts, operands, rows, width, extra_outs, flops):
    vmem = pl.BlockSpec(memory_space=pltpu.VMEM)
    outs = [pltpu.VMEM((rows, width), jnp.float32)]
    outs += [pltpu.VMEM((rows, width), jnp.bfloat16)] * (LINE - 1) + extra_outs
    return pl.pallas_call(
        kernel,
        in_specs=[pl.BlockSpec(memory_space=pltpu.SMEM)]
        + [pl.BlockSpec(memory_space=pl.ANY)] * len(parts)
        + [vmem] * len(operands),
        out_specs=[vmem] * len(outs),
        out_shape=outs,
        scratch_shapes=[
            pltpu.SemaphoreType.DMA((LINE,)),
            pltpu.VMEM((LINE * rows, parts[0].shape[1]), jnp.bfloat16),
            pltpu.VMEM((LINE * rows, width), jnp.float32),
        ],
        compiler_params=pltpu.CompilerParams(vmem_limit_bytes=16 * 2**20),
        cost_estimate=pl.CostEstimate(flops=flops, bytes_accessed=0, transcendentals=0),
        name=name,
    )(where, *parts, *[in_vmem(value) for value in operands])


def exchange_sum(value, axis, step):
    pairs = [(i, i ^ step) for i in range(lax.axis_size(axis))]
    return value + lax.ppermute(value, axis, pairs)


def gate_pieces(routes, gates, owners):
    rest = jnp.sum(
        jnp.where(
            routes[:, :, None] == jnp.arange(owners, dtype=jnp.int32)[None, None, :],
            gates[:, :, None],
            jnp.float32(0.0),
        ),
        axis=1,
    )
    pieces = []
    for _ in range(GATE_PIECES):
        piece = lax.reduce_precision(rest, 8, 7)
        pieces.append(piece.astype(jnp.bfloat16))
        rest = rest - piece
    return jnp.pad(jnp.concatenate(pieces, axis=1), ((0, 0), (0, LANES - GATE_PIECES * owners)))


def line_shards(tokens, tangent, routes, gates, w_gate, w_up, w_down):
    token_count, width = tokens.shape
    hidden = w_gate.shape[2]
    owners = lax.axis_size("expert")
    me = lax.axis_index("expert")
    pos = me // CORES
    inner = (pos == 1) | (pos == 2)
    where = jnp.stack([inner.astype(jnp.int32), me, me ^ 1])
    half = token_count // 2
    line_rows = LINE * half
    swap = [(i, i ^ 1) for i in range(owners)]

    def pick(ends, inners):
        return jnp.where(inner, inners, ends)

    def home(parts, side, inner_last):
        return parts[0] + side.astype(jnp.float32) + pick(0.0, inner_last.astype(jnp.float32))

    def forward(parts):
        state = pltpu.VMEM((line_rows, CORES * hidden), jnp.float32)
        *outs, b_slope, act = kernel_call(
            functools.partial(forward_kernel, owners),
            "forward",
            where,
            parts,
            weights,
            half,
            width,
            [state, state],
            2 * 5 * line_rows * width * CORES * hidden,
        )
        return outs, (b_slope, act)

    def backward(parts, states):
        *outs, squares = kernel_call(
            backward_kernel,
            "backward",
            where,
            parts,
            (*states, *weights),
            half,
            width,
            [pltpu.VMEM((8, LANES), jnp.float32)],
            2 * 3 * line_rows * width * CORES * hidden,
        )
        return outs, squares

    pieces = gate_pieces(routes, gates, owners)
    halves = [slice(0, half), slice(half, token_count)]
    load_a, load_b = (
        jnp.concatenate([tokens[rows], tangent[rows], pieces[rows]], axis=1) for rows in halves
    )

    def slot(*results):
        return lax.optimization_barrier(results)

    def both_ways(part, payload):
        first = pick(part, payload[:, :width])
        if payload.shape[1] > width:
            first = jnp.concatenate([first, payload[:, width:]], axis=1)
        return side_hop(first)

    a_side, a_near, sib_gate, w_up, w_down, load_b = slot(
        side_hop(load_a), inner_hop(load_a), lax.ppermute(w_gate, "expert", swap), w_up, w_down, load_b
    )
    a_near_end, a_far, sib_up, w_down, load_b = slot(
        side_hop(a_near), inner_hop(a_side), lax.ppermute(w_up, "expert", swap), w_down, load_b
    )
    a_far_end, sib_down, load_b = slot(side_hop(a_far), lax.ppermute(w_down, "expert", swap), load_b)
    weights = (w_gate, w_up, w_down, sib_gate, sib_up, sib_down)

    b_side, b_near, (pa, states_a) = slot(
        side_hop(load_b),
        inner_hop(load_b),
        forward((load_a, a_side, a_near, a_near_end, a_far, a_far_end)),
    )
    b_near_end, b_far = slot(both_ways(pa[3], b_near), inner_hop(b_side))
    sa_far = add_rows(pa[3], b_near_end[:, :width])
    b_far_end, sa_side = slot(both_ways(pa[2], b_far), inner_hop(sa_far))
    sa_near = add_rows(pa[2], b_far_end[:, :width])
    came, last, (pb, states_b) = slot(
        both_ways(pa[1], add_rows(pa[1], sa_side)),
        inner_hop(sa_near),
        forward((load_b, b_side, b_near, b_near_end, b_far, b_far_end)),
    )
    jv_a = tangent[:half].astype(jnp.float32) + home(pa, came, last)

    def gather_and_reduce(own, parts, work):
        side, near = slot(side_hop(own), inner_hop(own))
        near_end, far = slot(both_ways(parts[3], near), inner_hop(side))
        s_far = add_rows(parts[3], near_end)
        far_end, s_side = slot(both_ways(parts[2], far), inner_hop(s_far))
        s_near = add_rows(parts[2], far_end)
        came, last, worked = slot(
            both_ways(parts[1], add_rows(parts[1], s_side)),
            inner_hop(s_near),
            work((own, side, near, near_end, far, far_end)),
        )
        return worked, home(parts, came, last)

    (ga, squares_a), sum_b = gather_and_reduce(
        jv_a.astype(jnp.bfloat16), pb, lambda parts: backward(parts, states_a)
    )
    jv_b = tangent[half:].astype(jnp.float32) + sum_b
    (gb, squares_b), grad_a = gather_and_reduce(
        jv_b.astype(jnp.bfloat16), ga, lambda parts: backward(parts, states_b)
    )

    sum_a = jv_a + grad_a
    lines = lax.axis_size("dp")
    first, second = side_hop(gb[3]), side_hop(gb[2])
    first, squares = slot(first, exchange_sum(squares_a + squares_b, "expert", 1))
    step = 1
    while step < lines // 2:
        squares = exchange_sum(squares, "dp", step)
        step *= 2
    s_near = add_rows(gb[2], second)
    s_side, second, squares = slot(inner_hop(add_rows(gb[3], first)), second, squares)
    came, last = side_hop(pick(gb[1], add_rows(gb[1], s_side))), inner_hop(s_near)
    while step < lines:
        squares = exchange_sum(squares, "dp", step)
        step *= 2
    grad_b = home(gb, came, last)

    elements = token_count * width * lax.axis_size("dp") * owners
    scale = lax.rsqrt(jnp.sum(squares[0]) / elements + 1e-06)
    return jnp.concatenate([sum_a * scale, (jv_b + grad_b) * scale])


def owner_states(x_rows, gate_w, up_w):
    pre_a = dot(x_rows, gate_w)
    pre_b = dot(x_rows, up_w)
    sigma = jax.nn.sigmoid(pre_a)
    act = pre_a * sigma
    slope = sigma * (1.0 + pre_a * (1.0 - sigma))
    return (pre_b, act, slope)


def pair_shards(tokens, tangent, routes, gates, w_gate, w_up, w_down):
    token_count, model_width = tokens.shape
    top_k = routes.shape[1]
    owners = lax.axis_size("expert")
    expert_total = owners * w_gate.shape[0]
    capacity = pair_capacity(token_count, top_k, expert_total)
    slot_total = expert_total * capacity
    pair_count = token_count * top_k
    gate_w = w_gate[0]
    up_w = w_up[0]
    down_w = w_down[0]
    flat_routes = routes.reshape(pair_count)
    onehot = (flat_routes[:, None] == jnp.arange(expert_total, dtype=jnp.int32)[None, :]).astype(
        jnp.int32
    )
    before = jnp.cumsum(onehot, axis=0) - onehot
    slot_of = jnp.sum(before * onehot, axis=1)
    slot_index = flat_routes * capacity + slot_of
    slot_match = slot_index[None, :] == jnp.arange(slot_total, dtype=jnp.int32)[:, None]
    filled = jnp.any(slot_match, axis=1)
    pair_token = jnp.arange(pair_count, dtype=jnp.int32) // top_k
    source_token = jnp.sum(jnp.where(slot_match, pair_token[None, :], 0), axis=1)
    source_gate = jnp.sum(
        jnp.where(slot_match, gates.reshape(pair_count)[None, :], jnp.float32(0.0)), axis=1
    )
    keep_mask = filled.astype(jnp.bfloat16)[:, None]

    def exchange(rows):
        blocks = rows.reshape(owners, capacity, model_width)
        moved = lax.all_to_all(blocks, "expert", split_axis=0, concat_axis=0, tiled=True)
        return moved.reshape(slot_total, model_width)

    x_rows = exchange(jnp.take(tokens, source_token, axis=0) * keep_mask)
    v_rows = exchange(jnp.take(tangent, source_token, axis=0) * keep_mask)
    pre_b, act, slope = owner_states(x_rows, gate_w, up_w)
    tan_a = dot(v_rows, gate_w)
    tan_b = dot(v_rows, up_w)
    hidden_tangent = (slope * tan_a * pre_b + act * tan_b).astype(jnp.bfloat16)
    returned = exchange(dot(hidden_tangent, down_w).astype(jnp.bfloat16))
    picked_rows = jnp.take(returned, slot_index, axis=0)
    picked_rows = picked_rows.reshape(token_count, top_k, model_width)
    jv_vals = tangent.astype(jnp.float32) + jnp.sum(
        gates[:, :, None] * picked_rows.astype(jnp.float32), axis=1
    )
    cot_rows = exchange(
        (jnp.take(jv_vals, source_token, axis=0) * source_gate[:, None]).astype(jnp.bfloat16)
    )
    back_vals = dot_last(cot_rows, down_w)
    grad_gate = (back_vals * pre_b * slope).astype(jnp.bfloat16)
    grad_up = (back_vals * act).astype(jnp.bfloat16)
    pair_grad = dot_last(grad_gate, gate_w) + dot_last(grad_up, up_w)
    grad_rows = jnp.take(exchange(pair_grad.astype(jnp.bfloat16)), slot_index, axis=0)
    grad_rows = grad_rows.reshape(token_count, top_k, model_width)
    summed = jv_vals + jnp.sum(grad_rows.astype(jnp.float32), axis=1)
    global_sum = lax.psum(jnp.sum(jv_vals * jv_vals), ("dp", "expert"))
    element_count = token_count * lax.axis_size("dp") * owners * model_width
    return summed * lax.rsqrt(global_sum / element_count + 1e-06)


def pair_capacity(token_count, top_k, expert_total):
    return max(2, token_count * top_k * 9 // (8 * expert_total))


def shards(tokens, tangent, routes, gates, w_gate, w_up, w_down):
    token_count, top_k = routes.shape
    owners = lax.axis_size("expert")
    capacity = pair_capacity(token_count, top_k, owners * w_gate.shape[0])
    dp = lax.axis_size("dp")
    whole_blocks = (
        owners == CORES * LINE
        and dp & (dp - 1) == 0
        and w_gate.shape[0] == 1
        and token_count <= CORES * capacity
    )
    form = line_shards if whole_blocks else pair_shards
    return form(tokens, tangent, routes, gates, w_gate, w_up, w_down)


def solution(mesh):
    placed = (
        P(("dp", "expert"), None),
        P(("dp", "expert"), None),
        P(("dp", "expert"), None),
        P(("dp", "expert"), None),
        P("expert", None, None),
        P("expert", None, None),
        P("expert", None, None),
    )
    return jax.shard_map(
        shards, mesh=mesh, in_specs=placed, out_specs=P(("dp", "expert"), None), check_vma=False
    )
```

```python
import functools

import jax
import jax.numpy as jnp
from jax import lax
from jax.experimental import pallas as pl
from jax.experimental.pallas import tpu as pltpu
from jax.sharding import PartitionSpec as P

CONTRACT_LAST = (((1,), (1,)), ((), ()))


def dot(lhs, rhs):
    return jnp.dot(lhs, rhs, preferred_element_type=jnp.float32)


def dot_last(lhs, rhs):
    return lax.dot_general(lhs, rhs, CONTRACT_LAST, preferred_element_type=jnp.float32)


CORES, SIDES, ENDS = 2, 2, 2
LINE = SIDES * ENDS
SIDE_PAIRS = ((0, 1), (1, 0), (2, 3), (3, 2))
INNER_PAIRS = ((1, 2), (2, 1))


END_CHIPS = (0, 3)


def both_cores(pairs):
    return [(CORES * a + core, CORES * b + core) for a, b in pairs for core in range(CORES)]


def side_hop(rows):
    return lax.ppermute(rows, "expert", both_cores(SIDE_PAIRS))


def inner_hop(rows):
    idle = [(CORES * a + core, CORES * a + 1 - core) for a in END_CHIPS for core in range(CORES)]
    return lax.ppermute(rows, "expert", both_cores(INNER_PAIRS) + idle)


def add_rows(own, came):
    return (own.astype(jnp.float32) + came.astype(jnp.float32)).astype(jnp.bfloat16)


def in_vmem(value):
    return pltpu.with_memory_space_constraint(value, pltpu.VMEM)


LANES = 128
GATE_PIECES = 3


def fetch(inner, parts, blocks, out, sems):
    own, side, near, near_end, far, far_end = parts
    rows = own.shape[0]
    chosen = ((own, side, near, far), (own, side, near_end, far_end))

    def copies(mine):
        return [
            pltpu.make_async_copy(mine[block], out.at[pl.ds(i * rows, rows), :], sems.at[i])
            for i, block in enumerate(blocks)
        ]

    def begin(mine):
        for copy in copies(mine):
            copy.start()

    def finish(mine):
        for copy in copies(mine):
            copy.wait()

    for act in (begin, finish):
        pl.when(inner)(functools.partial(act, chosen[0]))
        pl.when(jnp.logical_not(inner))(functools.partial(act, chosen[1]))


def add_term(total, earlier, term):
    total[...] = term if earlier is None else earlier[...] + term


def store_parts(total, outs):
    for i, out in enumerate(outs):
        rows = out.shape[0]
        out[...] = total[pl.ds(i * rows, rows), :].astype(out.dtype)


def forward_kernel(owners, experts, start, finish, unused, where_ref, *refs):
    refs = list(refs[unused:])
    parts, refs = refs[:6], refs[6:]
    earlier = None if start else refs.pop(0)
    weights, refs = refs[: 3 * len(experts)], refs[3 * len(experts) :]
    sems, load, total = refs[-3:]
    states = refs[-3 - 2 * len(experts) : -3]
    outs = refs[: -3 - 2 * len(experts)]
    if not finish:
        total = outs[0]
    width = total.shape[1]
    fetch(where_ref[0] == 1, parts, range(LINE), load, sems)
    x, v = load.at[:, pl.ds(0, width)], load.at[:, pl.ds(width, width)]
    gates = load.at[:, pl.ds(2 * width, LANES)]
    lane = lax.broadcasted_iota(jnp.int32, (1, LANES), 1)
    for i, which in enumerate(experts):
        gate_w, up_w, down_w = weights[3 * i : 3 * i + 3]
        expert = where_ref[1 + which]
        named = lane == expert
        for piece in range(1, GATE_PIECES):
            named = named | (lane == expert + piece * owners)
        g = jnp.sum(jnp.where(named, gates[...].astype(jnp.float32), 0.0), axis=1, keepdims=True)
        a, b = dot(x[...], gate_w[0]), dot(x[...], up_w[0])
        da, db = dot(v[...], gate_w[0]), dot(v[...], up_w[0])
        sigma = 1.0 / (1.0 + jnp.exp(-a))
        act = g * (a * sigma)
        b_slope = g * (sigma * (1.0 + a * (1.0 - sigma))) * b
        states[2 * i][...] = b_slope
        states[2 * i + 1][...] = act
        term = dot((b_slope * da + act * db).astype(jnp.bfloat16), down_w[0])
        add_term(total, earlier, term)
        earlier = total
    if finish:
        store_parts(total, outs)


def backward_kernel(experts, blocks, start, finish, unused, where_ref, *refs):
    refs = list(refs[unused:])
    parts, refs = refs[:6], refs[6:]
    earlier = None if start else refs.pop(0)
    states, refs = refs[: 2 * len(experts)], refs[2 * len(experts) :]
    weights, refs = refs[: 3 * len(experts)], refs[3 * len(experts) :]
    sems, jv, total = refs[-3:]
    outs = refs[:-3]
    squares = outs.pop() if start else None
    if not finish:
        total = outs[0]
    rows = parts[0].shape[0]
    here = pl.ds(blocks[0] * rows, len(blocks) * rows)
    fetch(where_ref[0] == 1, parts, blocks, jv, sems)
    if start:
        sums = jnp.zeros((1, LANES), jnp.float32)
        for column in range(0, jv.shape[1], LANES):
            piece = jv[:, pl.ds(column, LANES)].astype(jnp.float32)
            sums = sums + jnp.sum(piece * piece, axis=0, keepdims=True)
        squares[...] = jnp.broadcast_to(sums, squares.shape)
    for i in range(len(experts)):
        gate_w, up_w, down_w = weights[3 * i : 3 * i + 3]
        back = dot_last(jv[...], down_w[0])
        grad_gate = (back * states[2 * i][here, :]).astype(jnp.bfloat16)
        grad_up = (back * states[2 * i + 1][here, :]).astype(jnp.bfloat16)
        term = dot_last(grad_gate, gate_w[0]) + dot_last(grad_up, up_w[0])
        add_term(total, earlier, term)
        earlier = total
    if finish:
        store_parts(total, outs)


def kernel_call(kernel, name, where, parts, operands, outs, blocks, width, flops, unused=()):
    anywhere, vmem = pl.BlockSpec(memory_space=pl.ANY), pl.BlockSpec(memory_space=pltpu.VMEM)
    called = functools.partial(kernel, len(unused))
    rows = parts[0].shape[0] * blocks
    return pl.pallas_call(
        called,
        in_specs=[pl.BlockSpec(memory_space=pltpu.SMEM)]
        + [anywhere] * (len(parts) + len(unused))
        + [vmem] * len(operands),
        out_specs=[vmem] * len(outs),
        out_shape=[pltpu.VMEM(shape, kind) for shape, kind in outs],
        scratch_shapes=[
            pltpu.SemaphoreType.DMA((blocks,)),
            pltpu.VMEM((rows, parts[0].shape[1]), jnp.bfloat16),
            pltpu.VMEM((rows, width), jnp.float32),
        ],
        compiler_params=pltpu.CompilerParams(vmem_limit_bytes=16 * 2**20),
        cost_estimate=pl.CostEstimate(flops=flops, bytes_accessed=0, transcendentals=0),
        name=name,
    )(where, *unused, *parts, *[in_vmem(value) for value in operands])


def touch_kernel(*refs):
    refs[-1][...] = refs[0][0, pl.ds(0, 16), pl.ds(0, LANES)]


def touch(weights):
    vmem = pl.BlockSpec(memory_space=pltpu.VMEM)
    return pl.pallas_call(
        touch_kernel,
        in_specs=[vmem] * len(weights),
        out_specs=vmem,
        out_shape=pltpu.VMEM((16, LANES), jnp.bfloat16),
        compiler_params=pltpu.CompilerParams(vmem_limit_bytes=12 * 2**20),
        name="touch",
    )(*[in_vmem(value) for value in weights])


def exchange_sum(value, axis, step):
    pairs = [(i, i ^ step) for i in range(lax.axis_size(axis))]
    return value + lax.ppermute(value, axis, pairs)


def gate_pieces(routes, gates, owners):
    rest = jnp.sum(
        jnp.where(
            routes[:, :, None] == jnp.arange(owners, dtype=jnp.int32)[None, None, :],
            gates[:, :, None],
            jnp.float32(0.0),
        ),
        axis=1,
    )
    pieces = []
    for _ in range(GATE_PIECES):
        piece = lax.reduce_precision(rest, 8, 7)
        pieces.append(piece.astype(jnp.bfloat16))
        rest = rest - piece
    return jnp.pad(jnp.concatenate(pieces, axis=1), ((0, 0), (0, LANES - GATE_PIECES * owners)))


def line_shards(tokens, tangent, routes, gates, w_gate, w_up, w_down):
    token_count, width = tokens.shape
    hidden = w_gate.shape[2]
    owners = lax.axis_size("expert")
    me = lax.axis_index("expert")
    pos = me // CORES
    inner = (pos == 1) | (pos == 2)
    where = jnp.stack([inner.astype(jnp.int32), me, me ^ 1])
    half = token_count // 2
    line_rows = LINE * half
    swap = [(i, i ^ 1) for i in range(owners)]

    def pick(ends, inners):
        return jnp.where(inner, inners, ends)

    def home(parts, side, inner_last):
        return parts[0] + side.astype(jnp.float32) + pick(0.0, inner_last.astype(jnp.float32))

    def part_outs(blocks):
        return [((half, width), jnp.float32 if block == 0 else jnp.bfloat16) for block in blocks]

    def forward(parts, experts, earlier=None, unused=()):
        finish = experts[-1] == CORES - 1
        outs = part_outs(range(LINE)) if finish else [((line_rows, width), jnp.float32)]
        result = kernel_call(
            functools.partial(forward_kernel, owners, experts, experts[0] == 0, finish),
            "forward",
            where,
            parts,
            ([] if earlier is None else [earlier]) + [w for e in experts for w in weights[e]],
            outs + [((line_rows, hidden), jnp.float32)] * (2 * len(experts)),
            LINE,
            width,
            2 * 5 * line_rows * width * hidden * len(experts),
            unused,
        )
        states = result[len(outs) :]
        return (result[: len(outs)] if finish else result[0]), states

    def backward(parts, states, experts, blocks=tuple(range(LINE)), earlier=None):
        start, finish = experts[0] == 0, experts[-1] == CORES - 1
        rows = len(blocks) * half
        outs = part_outs(blocks) if finish else [((rows, width), jnp.float32)]
        result = kernel_call(
            functools.partial(backward_kernel, experts, blocks, start, finish),
            "backward",
            where,
            parts,
            ([] if earlier is None else [earlier])
            + [s for e in experts for s in states[2 * e : 2 * e + 2]]
            + [w for e in experts for w in weights[e]],
            outs + ([((8, LANES), jnp.float32)] if start else []),
            len(blocks),
            width,
            2 * 3 * rows * width * hidden * len(experts),
        )
        squares = result[-1] if start else None
        return (result[: len(outs)] if finish else result[0]), squares

    pieces = gate_pieces(routes, gates, owners)
    halves = [slice(0, half), slice(half, token_count)]
    load_a, load_b = (
        jnp.concatenate([tokens[rows], tangent[rows], pieces[rows]], axis=1) for rows in halves
    )

    def slot(*results):
        return lax.optimization_barrier(results)

    def both_ways(part, payload):
        first = pick(part, payload[:, :width])
        if payload.shape[1] > width:
            first = jnp.concatenate([first, payload[:, width:]], axis=1)
        return side_hop(first)

    a_side, a_near, sib_gate, w_up, w_down, load_b = slot(
        side_hop(load_a), inner_hop(load_a), lax.ppermute(w_gate, "expert", swap), w_up, w_down, load_b
    )
    a_near_end, a_far, sib_up, own_piece, w_down, load_b = slot(
        side_hop(a_near),
        inner_hop(a_side),
        lax.ppermute(w_up, "expert", swap),
        touch((w_gate, w_up, w_down)),
        w_down,
        load_b,
    )
    a_far_end, sib_down, sib_piece, load_b = slot(
        side_hop(a_far), lax.ppermute(w_down, "expert", swap), touch((sib_gate, sib_up)), load_b
    )
    weights = ((w_gate, w_up, w_down), (sib_gate, sib_up, sib_down))

    everyone = tuple(range(CORES))
    b_side, b_near, (pa, states_a) = slot(
        side_hop(load_b),
        inner_hop(load_b),
        forward(
            (load_a, a_side, a_near, a_near_end, a_far, a_far_end), everyone, unused=(own_piece, sib_piece)
        ),
    )
    b_near_end, b_far = slot(both_ways(pa[3], b_near), inner_hop(b_side))
    sa_far = add_rows(pa[3], b_near_end[:, :width])
    b_far_end, sa_side = slot(both_ways(pa[2], b_far), inner_hop(sa_far))
    sa_near = add_rows(pa[2], b_far_end[:, :width])
    b_parts = (load_b, b_side, b_near, b_near_end, b_far, b_far_end)
    came, last, (sum_b, states_b) = slot(
        both_ways(pa[1], add_rows(pa[1], sa_side)), inner_hop(sa_near), forward(b_parts, everyone[:1])
    )
    jv_a = tangent[:half].astype(jnp.float32) + home(pa, came, last)

    ja = jv_a.astype(jnp.bfloat16)
    side, near, (pb, rest_b) = slot(
        side_hop(ja), inner_hop(ja), forward(b_parts, everyone[1:], sum_b)
    )
    states_b = [*states_b, *rest_b]
    near_end, far = slot(both_ways(pb[3], near), inner_hop(side))
    s_far = add_rows(pb[3], near_end)
    far_end, s_side = slot(both_ways(pb[2], far), inner_hop(s_far))
    s_near = add_rows(pb[2], far_end)
    ja_parts = (ja, side, near, near_end, far, far_end)
    came, last, (sum_a, squares_a) = slot(
        both_ways(pb[1], add_rows(pb[1], s_side)),
        inner_hop(s_near),
        backward(ja_parts, states_a, everyone[:1]),
    )
    jv_b = tangent[half:].astype(jnp.float32) + home(pb, came, last)

    jb = jv_b.astype(jnp.bfloat16)
    side, near, (ga, _) = slot(
        side_hop(jb), inner_hop(jb), backward(ja_parts, states_a, everyone[1:], earlier=sum_a)
    )
    near_end, far = slot(both_ways(ga[3], near), inner_hop(side))
    s_far = add_rows(ga[3], near_end)
    far_end, s_side = slot(both_ways(ga[2], far), inner_hop(s_far))
    s_near = add_rows(ga[2], far_end)
    jb_parts = (jb, side, near, near_end, far, far_end)
    came, last, (gb, squares_b) = slot(
        both_ways(ga[1], add_rows(ga[1], s_side)),
        inner_hop(s_near),
        backward(jb_parts, states_b, everyone),
    )
    whole_a = jv_a + home(ga, came, last)

    lines = lax.axis_size("dp")
    squares = exchange_sum(squares_a + squares_b, "expert", 1)
    step = 1
    while step < lines // 2:
        squares = exchange_sum(squares, "dp", step)
        step *= 2
    came, squares = slot(side_hop(gb[3]), squares)
    came, s_side = slot(side_hop(gb[2]), inner_hop(add_rows(gb[3], came)))
    s_near = add_rows(gb[2], came)
    while step < lines:
        squares = exchange_sum(squares, "dp", step)
        step *= 2
    came, last = side_hop(pick(gb[1], add_rows(gb[1], s_side))), inner_hop(s_near)
    grad_b = home(gb, came, last)

    elements = token_count * width * lax.axis_size("dp") * owners
    scale = lax.rsqrt(jnp.sum(squares[0]) / elements + 1e-06)
    return jnp.concatenate([whole_a * scale, (jv_b + grad_b) * scale])


def owner_states(x_rows, gate_w, up_w):
    pre_a = dot(x_rows, gate_w)
    pre_b = dot(x_rows, up_w)
    sigma = jax.nn.sigmoid(pre_a)
    act = pre_a * sigma
    slope = sigma * (1.0 + pre_a * (1.0 - sigma))
    return (pre_b, act, slope)


def pair_shards(tokens, tangent, routes, gates, w_gate, w_up, w_down):
    token_count, model_width = tokens.shape
    top_k = routes.shape[1]
    owners = lax.axis_size("expert")
    expert_total = owners * w_gate.shape[0]
    capacity = pair_capacity(token_count, top_k, expert_total)
    slot_total = expert_total * capacity
    pair_count = token_count * top_k
    gate_w = w_gate[0]
    up_w = w_up[0]
    down_w = w_down[0]
    flat_routes = routes.reshape(pair_count)
    onehot = (flat_routes[:, None] == jnp.arange(expert_total, dtype=jnp.int32)[None, :]).astype(
        jnp.int32
    )
    before = jnp.cumsum(onehot, axis=0) - onehot
    slot_of = jnp.sum(before * onehot, axis=1)
    slot_index = flat_routes * capacity + slot_of
    slot_match = slot_index[None, :] == jnp.arange(slot_total, dtype=jnp.int32)[:, None]
    filled = jnp.any(slot_match, axis=1)
    pair_token = jnp.arange(pair_count, dtype=jnp.int32) // top_k
    source_token = jnp.sum(jnp.where(slot_match, pair_token[None, :], 0), axis=1)
    source_gate = jnp.sum(
        jnp.where(slot_match, gates.reshape(pair_count)[None, :], jnp.float32(0.0)), axis=1
    )
    keep_mask = filled.astype(jnp.bfloat16)[:, None]

    def exchange(rows):
        blocks = rows.reshape(owners, capacity, model_width)
        moved = lax.all_to_all(blocks, "expert", split_axis=0, concat_axis=0, tiled=True)
        return moved.reshape(slot_total, model_width)

    x_rows = exchange(jnp.take(tokens, source_token, axis=0) * keep_mask)
    v_rows = exchange(jnp.take(tangent, source_token, axis=0) * keep_mask)
    pre_b, act, slope = owner_states(x_rows, gate_w, up_w)
    tan_a = dot(v_rows, gate_w)
    tan_b = dot(v_rows, up_w)
    hidden_tangent = (slope * tan_a * pre_b + act * tan_b).astype(jnp.bfloat16)
    returned = exchange(dot(hidden_tangent, down_w).astype(jnp.bfloat16))
    picked_rows = jnp.take(returned, slot_index, axis=0)
    picked_rows = picked_rows.reshape(token_count, top_k, model_width)
    jv_vals = tangent.astype(jnp.float32) + jnp.sum(
        gates[:, :, None] * picked_rows.astype(jnp.float32), axis=1
    )
    cot_rows = exchange(
        (jnp.take(jv_vals, source_token, axis=0) * source_gate[:, None]).astype(jnp.bfloat16)
    )
    back_vals = dot_last(cot_rows, down_w)
    grad_gate = (back_vals * pre_b * slope).astype(jnp.bfloat16)
    grad_up = (back_vals * act).astype(jnp.bfloat16)
    pair_grad = dot_last(grad_gate, gate_w) + dot_last(grad_up, up_w)
    grad_rows = jnp.take(exchange(pair_grad.astype(jnp.bfloat16)), slot_index, axis=0)
    grad_rows = grad_rows.reshape(token_count, top_k, model_width)
    summed = jv_vals + jnp.sum(grad_rows.astype(jnp.float32), axis=1)
    global_sum = lax.psum(jnp.sum(jv_vals * jv_vals), ("dp", "expert"))
    element_count = token_count * lax.axis_size("dp") * owners * model_width
    return summed * lax.rsqrt(global_sum / element_count + 1e-06)


def pair_capacity(token_count, top_k, expert_total):
    return max(2, token_count * top_k * 9 // (8 * expert_total))


def shards(tokens, tangent, routes, gates, w_gate, w_up, w_down):
    token_count, top_k = routes.shape
    owners = lax.axis_size("expert")
    capacity = pair_capacity(token_count, top_k, owners * w_gate.shape[0])
    dp = lax.axis_size("dp")
    whole_blocks = (
        owners == CORES * LINE
        and dp & (dp - 1) == 0
        and w_gate.shape[0] == 1
        and token_count <= CORES * capacity
    )
    form = line_shards if whole_blocks else pair_shards
    return form(tokens, tangent, routes, gates, w_gate, w_up, w_down)


def solution(mesh):
    placed = (
        P(("dp", "expert"), None),
        P(("dp", "expert"), None),
        P(("dp", "expert"), None),
        P(("dp", "expert"), None),
        P("expert", None, None),
        P("expert", None, None),
        P("expert", None, None),
    )
    return jax.shard_map(
        shards, mesh=mesh, in_specs=placed, out_specs=P(("dp", "expert"), None), check_vma=False
    )
```

```python
import functools

import jax
import jax.numpy as jnp
from jax import lax
from jax.experimental import pallas as pl
from jax.experimental.pallas import tpu as pltpu
from jax.sharding import PartitionSpec as P

CONTRACT_LAST = (((1,), (1,)), ((), ()))


def dot(lhs, rhs):
    return jnp.dot(lhs, rhs, preferred_element_type=jnp.float32)


def dot_last(lhs, rhs):
    return lax.dot_general(lhs, rhs, CONTRACT_LAST, preferred_element_type=jnp.float32)


CORES, SIDES, ENDS = 2, 2, 2
LINE = SIDES * ENDS
SIDE_PAIRS = ((0, 1), (1, 0), (2, 3), (3, 2))
INNER_PAIRS = ((1, 2), (2, 1))


END_CHIPS = (0, 3)


def both_cores(pairs):
    return [(CORES * a + core, CORES * b + core) for a, b in pairs for core in range(CORES)]


def side_hop(rows):
    return lax.ppermute(rows, "expert", both_cores(SIDE_PAIRS))


def inner_hop(rows):
    idle = [(CORES * a + core, CORES * a + 1 - core) for a in END_CHIPS for core in range(CORES)]
    return lax.ppermute(rows, "expert", both_cores(INNER_PAIRS) + idle)


def add_rows(own, came):
    return (own.astype(jnp.float32) + came.astype(jnp.float32)).astype(jnp.bfloat16)


def in_vmem(value):
    return pltpu.with_memory_space_constraint(value, pltpu.VMEM)


LANES = 128
GATE_PIECES = 3


def fetch(inner, parts, blocks, out, sems):
    own, side, near, near_end, far, far_end = parts
    rows = own.shape[0]
    chosen = ((own, side, near, far), (own, side, near_end, far_end))

    def copies(mine):
        return [
            pltpu.make_async_copy(mine[block], out.at[pl.ds(i * rows, rows), :], sems.at[i])
            for i, block in enumerate(blocks)
        ]

    def begin(mine):
        for copy in copies(mine):
            copy.start()

    def finish(mine):
        for copy in copies(mine):
            copy.wait()

    for act in (begin, finish):
        pl.when(inner)(functools.partial(act, chosen[0]))
        pl.when(jnp.logical_not(inner))(functools.partial(act, chosen[1]))


def add_term(total, earlier, term):
    total[...] = term if earlier is None else earlier[...] + term


def store_parts(total, outs):
    for i, out in enumerate(outs):
        rows = out.shape[0]
        out[...] = total[pl.ds(i * rows, rows), :].astype(out.dtype)


def forward_kernel(owners, experts, start, finish, unused, where_ref, *refs):
    refs = list(refs[unused:])
    parts, refs = refs[:6], refs[6:]
    earlier = None if start else refs.pop(0)
    weights, refs = refs[: 3 * len(experts)], refs[3 * len(experts) :]
    sems, load, total = refs[-3:]
    states = refs[-3 - 2 * len(experts) : -3]
    outs = refs[: -3 - 2 * len(experts)]
    if not finish:
        total = outs[0]
    width = total.shape[1]
    fetch(where_ref[0] == 1, parts, range(LINE), load, sems)
    x, v = load.at[:, pl.ds(0, width)], load.at[:, pl.ds(width, width)]
    gates = load.at[:, pl.ds(2 * width, LANES)]
    lane = lax.broadcasted_iota(jnp.int32, (1, LANES), 1)
    for i, which in enumerate(experts):
        gate_w, up_w, down_w = weights[3 * i : 3 * i + 3]
        expert = where_ref[1 + which]
        named = lane == expert
        for piece in range(1, GATE_PIECES):
            named = named | (lane == expert + piece * owners)
        g = jnp.sum(jnp.where(named, gates[...].astype(jnp.float32), 0.0), axis=1, keepdims=True)
        a, b = dot(x[...], gate_w[0]), dot(x[...], up_w[0])
        da, db = dot(v[...], gate_w[0]), dot(v[...], up_w[0])
        sigma = 1.0 / (1.0 + jnp.exp(-a))
        act = g * (a * sigma)
        b_slope = g * (sigma * (1.0 + a * (1.0 - sigma))) * b
        states[2 * i][...] = b_slope
        states[2 * i + 1][...] = act
        term = dot((b_slope * da + act * db).astype(jnp.bfloat16), down_w[0])
        add_term(total, earlier, term)
        earlier = total
    if finish:
        store_parts(total, outs)


def backward_kernel(experts, blocks, start, finish, unused, where_ref, *refs):
    refs = list(refs[unused:])
    parts, refs = refs[:6], refs[6:]
    earlier = None if start else refs.pop(0)
    states, refs = refs[: 2 * len(experts)], refs[2 * len(experts) :]
    weights, refs = refs[: 3 * len(experts)], refs[3 * len(experts) :]
    sems, jv, total = refs[-3:]
    outs = refs[:-3]
    squares = outs.pop() if start else None
    if not finish:
        total = outs[0]
    rows = parts[0].shape[0]
    here = pl.ds(blocks[0] * rows, len(blocks) * rows)
    fetch(where_ref[0] == 1, parts, blocks, jv, sems)
    if start:
        sums = jnp.zeros((1, LANES), jnp.float32)
        for column in range(0, jv.shape[1], LANES):
            piece = jv[:, pl.ds(column, LANES)].astype(jnp.float32)
            sums = sums + jnp.sum(piece * piece, axis=0, keepdims=True)
        squares[...] = jnp.broadcast_to(sums, squares.shape)
    for i in range(len(experts)):
        gate_w, up_w, down_w = weights[3 * i : 3 * i + 3]
        back = dot_last(jv[...], down_w[0])
        grad_gate = (back * states[2 * i][here, :]).astype(jnp.bfloat16)
        grad_up = (back * states[2 * i + 1][here, :]).astype(jnp.bfloat16)
        term = dot_last(grad_gate, gate_w[0]) + dot_last(grad_up, up_w[0])
        add_term(total, earlier, term)
        earlier = total
    if finish:
        store_parts(total, outs)


def kernel_call(kernel, name, where, parts, operands, outs, blocks, width, flops, unused=()):
    anywhere, vmem = pl.BlockSpec(memory_space=pl.ANY), pl.BlockSpec(memory_space=pltpu.VMEM)
    called = functools.partial(kernel, len(unused))
    rows = parts[0].shape[0] * blocks
    return pl.pallas_call(
        called,
        in_specs=[pl.BlockSpec(memory_space=pltpu.SMEM)]
        + [anywhere] * (len(parts) + len(unused))
        + [vmem] * len(operands),
        out_specs=[vmem] * len(outs),
        out_shape=[pltpu.VMEM(shape, kind) for shape, kind in outs],
        scratch_shapes=[
            pltpu.SemaphoreType.DMA((blocks,)),
            pltpu.VMEM((rows, parts[0].shape[1]), jnp.bfloat16),
            pltpu.VMEM((rows, width), jnp.float32),
        ],
        compiler_params=pltpu.CompilerParams(vmem_limit_bytes=16 * 2**20),
        cost_estimate=pl.CostEstimate(flops=flops, bytes_accessed=0, transcendentals=0),
        name=name,
    )(where, *unused, *parts, *[in_vmem(value) for value in operands])


def output_kernel(elements, where_ref, squares, whole_a, jv_b, own, side, inner_last, out):
    scale = lax.rsqrt(jnp.sum(squares[pl.ds(0, 1), :], axis=1, keepdims=True) / elements + 1e-06)
    half = whole_a.shape[0]
    out[pl.ds(0, half), :] = whole_a[...] * scale
    total = jv_b[...] + own[...] + side[...].astype(jnp.float32)
    inner = where_ref[0] == 1

    @pl.when(inner)
    def _():
        out[pl.ds(half, half), :] = (total + inner_last[...].astype(jnp.float32)) * scale

    @pl.when(jnp.logical_not(inner))
    def _():
        out[pl.ds(half, half), :] = total * scale


def touch_kernel(*refs):
    refs[-1][...] = refs[0][0, pl.ds(0, 16), pl.ds(0, LANES)]


def touch(weights):
    vmem = pl.BlockSpec(memory_space=pltpu.VMEM)
    return pl.pallas_call(
        touch_kernel,
        in_specs=[vmem] * len(weights),
        out_specs=vmem,
        out_shape=pltpu.VMEM((16, LANES), jnp.bfloat16),
        compiler_params=pltpu.CompilerParams(vmem_limit_bytes=12 * 2**20),
        name="touch",
    )(*[in_vmem(value) for value in weights])


def exchange_sum(value, axis, step):
    pairs = [(i, i ^ step) for i in range(lax.axis_size(axis))]
    return value + lax.ppermute(value, axis, pairs)


def gate_pieces(routes, gates, owners):
    rest = jnp.sum(
        jnp.where(
            routes[:, :, None] == jnp.arange(owners, dtype=jnp.int32)[None, None, :],
            gates[:, :, None],
            jnp.float32(0.0),
        ),
        axis=1,
    )
    pieces = []
    for _ in range(GATE_PIECES):
        piece = lax.reduce_precision(rest, 8, 7)
        pieces.append(piece.astype(jnp.bfloat16))
        rest = rest - piece
    return jnp.pad(jnp.concatenate(pieces, axis=1), ((0, 0), (0, LANES - GATE_PIECES * owners)))


def line_shards(tokens, tangent, routes, gates, w_gate, w_up, w_down):
    token_count, width = tokens.shape
    hidden = w_gate.shape[2]
    owners = lax.axis_size("expert")
    me = lax.axis_index("expert")
    pos = me // CORES
    inner = (pos == 1) | (pos == 2)
    where = jnp.stack([inner.astype(jnp.int32), me, me ^ 1])
    half = token_count // 2
    line_rows = LINE * half
    swap = [(i, i ^ 1) for i in range(owners)]

    def pick(ends, inners):
        return jnp.where(inner, inners, ends)

    def home(parts, side, inner_last):
        return parts[0] + side.astype(jnp.float32) + pick(0.0, inner_last.astype(jnp.float32))

    def part_outs(blocks):
        return [((half, width), jnp.float32 if block == 0 else jnp.bfloat16) for block in blocks]

    def forward(parts, experts, earlier=None, unused=()):
        finish = experts[-1] == CORES - 1
        outs = part_outs(range(LINE)) if finish else [((line_rows, width), jnp.float32)]
        result = kernel_call(
            functools.partial(forward_kernel, owners, experts, experts[0] == 0, finish),
            "forward",
            where,
            parts,
            ([] if earlier is None else [earlier]) + [w for e in experts for w in weights[e]],
            outs + [((line_rows, hidden), jnp.float32)] * (2 * len(experts)),
            LINE,
            width,
            2 * 5 * line_rows * width * hidden * len(experts),
            unused,
        )
        states = result[len(outs) :]
        return (result[: len(outs)] if finish else result[0]), states

    def backward(parts, states, experts, blocks=tuple(range(LINE)), earlier=None):
        start, finish = experts[0] == 0, experts[-1] == CORES - 1
        rows = len(blocks) * half
        outs = part_outs(blocks) if finish else [((rows, width), jnp.float32)]
        result = kernel_call(
            functools.partial(backward_kernel, experts, blocks, start, finish),
            "backward",
            where,
            parts,
            ([] if earlier is None else [earlier])
            + [s for e in experts for s in states[2 * e : 2 * e + 2]]
            + [w for e in experts for w in weights[e]],
            outs + ([((8, LANES), jnp.float32)] if start else []),
            len(blocks),
            width,
            2 * 3 * rows * width * hidden * len(experts),
        )
        squares = result[-1] if start else None
        return (result[: len(outs)] if finish else result[0]), squares

    pieces = gate_pieces(routes, gates, owners)
    halves = [slice(0, half), slice(half, token_count)]
    load_a, load_b = (
        jnp.concatenate([tokens[rows], tangent[rows], pieces[rows]], axis=1) for rows in halves
    )

    def slot(*results):
        return lax.optimization_barrier(results)

    def both_ways(part, payload):
        first = pick(part, payload[:, :width])
        if payload.shape[1] > width:
            first = jnp.concatenate([first, payload[:, width:]], axis=1)
        return side_hop(first)

    a_side, a_near, sib_gate, w_up, w_down, load_b = slot(
        side_hop(load_a), inner_hop(load_a), lax.ppermute(w_gate, "expert", swap), w_up, w_down, load_b
    )
    a_near_end, a_far, sib_up, own_piece, w_down, load_b = slot(
        side_hop(a_near),
        inner_hop(a_side),
        lax.ppermute(w_up, "expert", swap),
        touch((w_gate, w_up, w_down)),
        w_down,
        load_b,
    )
    a_far_end, sib_down, sib_piece, load_b = slot(
        side_hop(a_far),
        lax.ppermute(w_down, "expert", swap),
        touch((sib_gate, sib_up, load_a, a_side, a_near, a_near_end, a_far)),
        load_b,
    )
    weights = ((w_gate, w_up, w_down), (sib_gate, sib_up, sib_down))

    everyone = tuple(range(CORES))
    b_side, b_near, (pa, states_a) = slot(
        side_hop(load_b),
        inner_hop(load_b),
        forward(
            (load_a, a_side, a_near, a_near_end, a_far, a_far_end), everyone, unused=(own_piece, sib_piece)
        ),
    )
    b_near_end, b_far = slot(both_ways(pa[3], b_near), inner_hop(b_side))
    sa_far = add_rows(pa[3], b_near_end[:, :width])
    b_far_end, sa_side = slot(both_ways(pa[2], b_far), inner_hop(sa_far))
    sa_near = add_rows(pa[2], b_far_end[:, :width])
    b_parts = (load_b, b_side, b_near, b_near_end, b_far, b_far_end)
    came, last, (sum_b, states_b) = slot(
        both_ways(pa[1], add_rows(pa[1], sa_side)), inner_hop(sa_near), forward(b_parts, everyone[:1])
    )
    jv_a = tangent[:half].astype(jnp.float32) + home(pa, came, last)

    ja = jv_a.astype(jnp.bfloat16)
    side, near, (pb, rest_b) = slot(
        side_hop(ja), inner_hop(ja), forward(b_parts, everyone[1:], sum_b)
    )
    states_b = [*states_b, *rest_b]
    near_end, far = slot(both_ways(pb[3], near), inner_hop(side))
    s_far = add_rows(pb[3], near_end)
    far_end, s_side = slot(both_ways(pb[2], far), inner_hop(s_far))
    s_near = add_rows(pb[2], far_end)
    ja_parts = (ja, side, near, near_end, far, far_end)
    came, last, (sum_a, squares_a) = slot(
        both_ways(pb[1], add_rows(pb[1], s_side)),
        inner_hop(s_near),
        backward(ja_parts, states_a, everyone[:1]),
    )
    jv_b = tangent[half:].astype(jnp.float32) + home(pb, came, last)

    jb = jv_b.astype(jnp.bfloat16)
    side, near, (ga, _) = slot(
        side_hop(jb), inner_hop(jb), backward(ja_parts, states_a, everyone[1:], earlier=sum_a)
    )
    near_end, far = slot(both_ways(ga[3], near), inner_hop(side))
    s_far = add_rows(ga[3], near_end)
    far_end, s_side = slot(both_ways(ga[2], far), inner_hop(s_far))
    s_near = add_rows(ga[2], far_end)
    jb_parts = (jb, side, near, near_end, far, far_end)
    came, last, (gb, squares_b) = slot(
        both_ways(ga[1], add_rows(ga[1], s_side)),
        inner_hop(s_near),
        backward(jb_parts, states_b, everyone),
    )
    whole_a = jv_a + home(ga, came, last)

    lines = lax.axis_size("dp")
    squares = exchange_sum(squares_a + squares_b, "expert", 1)
    step = 1
    while step < lines // 2:
        squares = exchange_sum(squares, "dp", step)
        step *= 2
    came, squares = slot(side_hop(gb[3]), squares)
    came, s_side = slot(side_hop(gb[2]), inner_hop(add_rows(gb[3], came)))
    s_near = add_rows(gb[2], came)
    while step < lines:
        squares = exchange_sum(squares, "dp", step)
        step *= 2
    came, last = side_hop(pick(gb[1], add_rows(gb[1], s_side))), inner_hop(s_near)
    vmem = pl.BlockSpec(memory_space=pltpu.VMEM)
    return pl.pallas_call(
        functools.partial(output_kernel, token_count * width * lines * owners),
        in_specs=[pl.BlockSpec(memory_space=pltpu.SMEM)] + [vmem] * 6,
        out_specs=vmem,
        out_shape=jax.ShapeDtypeStruct((token_count, width), jnp.float32),
        compiler_params=pltpu.CompilerParams(vmem_limit_bytes=8 * 2**20),
        name="output",
    )(where, *[in_vmem(value) for value in (squares, whole_a, jv_b, gb[0], came, last)])


def owner_states(x_rows, gate_w, up_w):
    pre_a = dot(x_rows, gate_w)
    pre_b = dot(x_rows, up_w)
    sigma = jax.nn.sigmoid(pre_a)
    act = pre_a * sigma
    slope = sigma * (1.0 + pre_a * (1.0 - sigma))
    return (pre_b, act, slope)


def pair_shards(tokens, tangent, routes, gates, w_gate, w_up, w_down):
    token_count, model_width = tokens.shape
    top_k = routes.shape[1]
    owners = lax.axis_size("expert")
    expert_total = owners * w_gate.shape[0]
    capacity = pair_capacity(token_count, top_k, expert_total)
    slot_total = expert_total * capacity
    pair_count = token_count * top_k
    gate_w = w_gate[0]
    up_w = w_up[0]
    down_w = w_down[0]
    flat_routes = routes.reshape(pair_count)
    onehot = (flat_routes[:, None] == jnp.arange(expert_total, dtype=jnp.int32)[None, :]).astype(
        jnp.int32
    )
    before = jnp.cumsum(onehot, axis=0) - onehot
    slot_of = jnp.sum(before * onehot, axis=1)
    slot_index = flat_routes * capacity + slot_of
    slot_match = slot_index[None, :] == jnp.arange(slot_total, dtype=jnp.int32)[:, None]
    filled = jnp.any(slot_match, axis=1)
    pair_token = jnp.arange(pair_count, dtype=jnp.int32) // top_k
    source_token = jnp.sum(jnp.where(slot_match, pair_token[None, :], 0), axis=1)
    source_gate = jnp.sum(
        jnp.where(slot_match, gates.reshape(pair_count)[None, :], jnp.float32(0.0)), axis=1
    )
    keep_mask = filled.astype(jnp.bfloat16)[:, None]

    def exchange(rows):
        blocks = rows.reshape(owners, capacity, model_width)
        moved = lax.all_to_all(blocks, "expert", split_axis=0, concat_axis=0, tiled=True)
        return moved.reshape(slot_total, model_width)

    x_rows = exchange(jnp.take(tokens, source_token, axis=0) * keep_mask)
    v_rows = exchange(jnp.take(tangent, source_token, axis=0) * keep_mask)
    pre_b, act, slope = owner_states(x_rows, gate_w, up_w)
    tan_a = dot(v_rows, gate_w)
    tan_b = dot(v_rows, up_w)
    hidden_tangent = (slope * tan_a * pre_b + act * tan_b).astype(jnp.bfloat16)
    returned = exchange(dot(hidden_tangent, down_w).astype(jnp.bfloat16))
    picked_rows = jnp.take(returned, slot_index, axis=0)
    picked_rows = picked_rows.reshape(token_count, top_k, model_width)
    jv_vals = tangent.astype(jnp.float32) + jnp.sum(
        gates[:, :, None] * picked_rows.astype(jnp.float32), axis=1
    )
    cot_rows = exchange(
        (jnp.take(jv_vals, source_token, axis=0) * source_gate[:, None]).astype(jnp.bfloat16)
    )
    back_vals = dot_last(cot_rows, down_w)
    grad_gate = (back_vals * pre_b * slope).astype(jnp.bfloat16)
    grad_up = (back_vals * act).astype(jnp.bfloat16)
    pair_grad = dot_last(grad_gate, gate_w) + dot_last(grad_up, up_w)
    grad_rows = jnp.take(exchange(pair_grad.astype(jnp.bfloat16)), slot_index, axis=0)
    grad_rows = grad_rows.reshape(token_count, top_k, model_width)
    summed = jv_vals + jnp.sum(grad_rows.astype(jnp.float32), axis=1)
    global_sum = lax.psum(jnp.sum(jv_vals * jv_vals), ("dp", "expert"))
    element_count = token_count * lax.axis_size("dp") * owners * model_width
    return summed * lax.rsqrt(global_sum / element_count + 1e-06)


def pair_capacity(token_count, top_k, expert_total):
    return max(2, token_count * top_k * 9 // (8 * expert_total))


def shards(tokens, tangent, routes, gates, w_gate, w_up, w_down):
    token_count, top_k = routes.shape
    owners = lax.axis_size("expert")
    capacity = pair_capacity(token_count, top_k, owners * w_gate.shape[0])
    dp = lax.axis_size("dp")
    whole_blocks = (
        owners == CORES * LINE
        and dp & (dp - 1) == 0
        and w_gate.shape[0] == 1
        and token_count <= CORES * capacity
    )
    form = line_shards if whole_blocks else pair_shards
    return form(tokens, tangent, routes, gates, w_gate, w_up, w_down)


def solution(mesh):
    placed = (
        P(("dp", "expert"), None),
        P(("dp", "expert"), None),
        P(("dp", "expert"), None),
        P(("dp", "expert"), None),
        P("expert", None, None),
        P("expert", None, None),
        P("expert", None, None),
    )
    return jax.shard_map(
        shards, mesh=mesh, in_specs=placed, out_specs=P(("dp", "expert"), None), check_vma=False
    )
```

```python
import functools

import jax
import jax.numpy as jnp
from jax import lax
from jax.experimental import pallas as pl
from jax.experimental.pallas import tpu as pltpu
from jax.sharding import PartitionSpec as P

CONTRACT_LAST = (((1,), (1,)), ((), ()))


def dot(lhs, rhs):
    return jnp.dot(lhs, rhs, preferred_element_type=jnp.float32)


def dot_last(lhs, rhs):
    return lax.dot_general(lhs, rhs, CONTRACT_LAST, preferred_element_type=jnp.float32)


CORES, SIDES, ENDS = 2, 2, 2
LINE = SIDES * ENDS
SIDE_PAIRS = ((0, 1), (1, 0), (2, 3), (3, 2))
INNER_PAIRS = ((1, 2), (2, 1))


END_CHIPS = (0, 3)


def both_cores(pairs):
    return [(CORES * a + core, CORES * b + core) for a, b in pairs for core in range(CORES)]


def side_hop(rows):
    return lax.ppermute(rows, "expert", both_cores(SIDE_PAIRS))


def inner_hop(rows):
    idle = [(CORES * a + core, CORES * a + 1 - core) for a in END_CHIPS for core in range(CORES)]
    return lax.ppermute(rows, "expert", both_cores(INNER_PAIRS) + idle)


def add_rows(own, came):
    return (own.astype(jnp.float32) + came.astype(jnp.float32)).astype(jnp.bfloat16)


def in_vmem(value):
    return pltpu.with_memory_space_constraint(value, pltpu.VMEM)


LANES = 128
GATE_PIECES = 3


def fetch(inner, parts, blocks, out, sems):
    own, side, near, near_end, far, far_end = parts
    rows = own.shape[0]
    chosen = ((own, side, near, far), (own, side, near_end, far_end))

    def copies(mine):
        return [
            pltpu.make_async_copy(mine[block], out.at[pl.ds(i * rows, rows), :], sems.at[i])
            for i, block in enumerate(blocks)
        ]

    def begin(mine):
        for copy in copies(mine):
            copy.start()

    def finish(mine):
        for copy in copies(mine):
            copy.wait()

    for act in (begin, finish):
        pl.when(inner)(functools.partial(act, chosen[0]))
        pl.when(jnp.logical_not(inner))(functools.partial(act, chosen[1]))


def add_term(total, earlier, term):
    total[...] = term if earlier is None else earlier[...] + term


def store_parts(total, outs):
    for i, out in enumerate(outs):
        rows = out.shape[0]
        out[...] = total[pl.ds(i * rows, rows), :].astype(out.dtype)


def forward_kernel(owners, experts, start, finish, where_ref, *refs):
    refs = list(refs)
    parts, refs = refs[:6], refs[6:]
    earlier = None if start else refs.pop(0)
    weights, refs = refs[: 3 * len(experts)], refs[3 * len(experts) :]
    sems, load, total = refs[-3:]
    states = refs[-3 - 2 * len(experts) : -3]
    outs = refs[: -3 - 2 * len(experts)]
    if not finish:
        total = outs[0]
    width = total.shape[1]
    fetch(where_ref[0] == 1, parts, range(LINE), load, sems)
    x, v = load.at[:, pl.ds(0, width)], load.at[:, pl.ds(width, width)]
    gates = load.at[:, pl.ds(2 * width, LANES)]
    lane = lax.broadcasted_iota(jnp.int32, (1, LANES), 1)
    for i, which in enumerate(experts):
        gate_w, up_w, down_w = weights[3 * i : 3 * i + 3]
        expert = where_ref[1 + which]
        named = lane == expert
        for piece in range(1, GATE_PIECES):
            named = named | (lane == expert + piece * owners)
        g = jnp.sum(jnp.where(named, gates[...].astype(jnp.float32), 0.0), axis=1, keepdims=True)
        a, b = dot(x[...], gate_w[0]), dot(x[...], up_w[0])
        da, db = dot(v[...], gate_w[0]), dot(v[...], up_w[0])
        sigma = 1.0 / (1.0 + jnp.exp(-a))
        act = g * (a * sigma)
        b_slope = g * (sigma * (1.0 + a * (1.0 - sigma))) * b
        states[2 * i][...] = b_slope
        states[2 * i + 1][...] = act
        term = dot((b_slope * da + act * db).astype(jnp.bfloat16), down_w[0])
        add_term(total, earlier, term)
        earlier = total
    if finish:
        store_parts(total, outs)


def backward_kernel(experts, blocks, start, finish, where_ref, *refs):
    refs = list(refs)
    parts, refs = refs[:6], refs[6:]
    earlier = None if start else refs.pop(0)
    states, refs = refs[: 2 * len(experts)], refs[2 * len(experts) :]
    weights, refs = refs[: 3 * len(experts)], refs[3 * len(experts) :]
    sems, jv, total = refs[-3:]
    outs = refs[:-3]
    squares = outs.pop() if start else None
    if not finish:
        total = outs[0]
    rows = parts[0].shape[0]
    here = pl.ds(blocks[0] * rows, len(blocks) * rows)
    fetch(where_ref[0] == 1, parts, blocks, jv, sems)
    if start:
        sums = jnp.zeros((1, LANES), jnp.float32)
        for column in range(0, jv.shape[1], LANES):
            piece = jv[:, pl.ds(column, LANES)].astype(jnp.float32)
            sums = sums + jnp.sum(piece * piece, axis=0, keepdims=True)
        squares[...] = jnp.broadcast_to(sums, squares.shape)
    for i in range(len(experts)):
        gate_w, up_w, down_w = weights[3 * i : 3 * i + 3]
        back = dot_last(jv[...], down_w[0])
        grad_gate = (back * states[2 * i][here, :]).astype(jnp.bfloat16)
        grad_up = (back * states[2 * i + 1][here, :]).astype(jnp.bfloat16)
        term = dot_last(grad_gate, gate_w[0]) + dot_last(grad_up, up_w[0])
        add_term(total, earlier, term)
        earlier = total
    if finish:
        store_parts(total, outs)


def kernel_call(kernel, name, where, parts, operands, outs, blocks, width, flops):
    anywhere, vmem = pl.BlockSpec(memory_space=pl.ANY), pl.BlockSpec(memory_space=pltpu.VMEM)
    rows = parts[0].shape[0] * blocks
    return pl.pallas_call(
        kernel,
        in_specs=[pl.BlockSpec(memory_space=pltpu.SMEM)]
        + [anywhere] * len(parts)
        + [vmem] * len(operands),
        out_specs=[vmem] * len(outs),
        out_shape=[pltpu.VMEM(shape, kind) for shape, kind in outs],
        scratch_shapes=[
            pltpu.SemaphoreType.DMA((blocks,)),
            pltpu.VMEM((rows, parts[0].shape[1]), jnp.bfloat16),
            pltpu.VMEM((rows, width), jnp.float32),
        ],
        compiler_params=pltpu.CompilerParams(vmem_limit_bytes=10 * 2**20),
        cost_estimate=pl.CostEstimate(flops=flops, bytes_accessed=0, transcendentals=0),
        name=name,
    )(where, *parts, *[in_vmem(value) for value in operands])


def output_kernel(elements, where_ref, squares, whole_a, jv_b, own, side, inner_last, out):
    scale = lax.rsqrt(jnp.sum(squares[pl.ds(0, 1), :], axis=1, keepdims=True) / elements + 1e-06)
    half = whole_a.shape[0]
    out[pl.ds(0, half), :] = whole_a[...] * scale
    total = jv_b[...] + own[...] + side[...].astype(jnp.float32)
    inner = where_ref[0] == 1

    @pl.when(inner)
    def _():
        out[pl.ds(half, half), :] = (total + inner_last[...].astype(jnp.float32)) * scale

    @pl.when(jnp.logical_not(inner))
    def _():
        out[pl.ds(half, half), :] = total * scale


def load_kernel(count, *refs):
    arrays, outs, sems = refs[:count], refs[count : 2 * count], refs[2 * count]
    copies = [
        pltpu.make_async_copy(array, out, sems.at[i]) for i, (array, out) in enumerate(zip(arrays, outs))
    ]
    for copy in copies:
        copy.start()
    for copy in copies:
        copy.wait()


def load(arrays):
    return pl.pallas_call(
        functools.partial(load_kernel, len(arrays)),
        in_specs=[pl.BlockSpec(memory_space=pl.ANY)] * len(arrays),
        out_specs=[pl.BlockSpec(memory_space=pltpu.VMEM)] * len(arrays),
        out_shape=[pltpu.VMEM(array.shape, array.dtype) for array in arrays],
        scratch_shapes=[pltpu.SemaphoreType.DMA((len(arrays),))],
        compiler_params=pltpu.CompilerParams(vmem_limit_bytes=2**20),
        name="load",
    )(*arrays)


def exchange_sum(value, axis, step):
    pairs = [(i, i ^ step) for i in range(lax.axis_size(axis))]
    return value + lax.ppermute(value, axis, pairs)


def gate_pieces(routes, gates, owners):
    rest = jnp.sum(
        jnp.where(
            routes[:, :, None] == jnp.arange(owners, dtype=jnp.int32)[None, None, :],
            gates[:, :, None],
            jnp.float32(0.0),
        ),
        axis=1,
    )
    pieces = []
    for _ in range(GATE_PIECES):
        piece = lax.reduce_precision(rest, 8, 7)
        pieces.append(piece.astype(jnp.bfloat16))
        rest = rest - piece
    return jnp.pad(jnp.concatenate(pieces, axis=1), ((0, 0), (0, LANES - GATE_PIECES * owners)))


def line_shards(tokens, tangent, routes, gates, w_gate, w_up, w_down):
    token_count, width = tokens.shape
    hidden = w_gate.shape[2]
    owners = lax.axis_size("expert")
    me = lax.axis_index("expert")
    pos = me // CORES
    inner = (pos == 1) | (pos == 2)
    where = jnp.stack([inner.astype(jnp.int32), me, me ^ 1])
    half = token_count // 2
    line_rows = LINE * half
    swap = [(i, i ^ 1) for i in range(owners)]

    def pick(ends, inners):
        return jnp.where(inner, inners, ends)

    def home(parts, side, inner_last):
        return parts[0] + side.astype(jnp.float32) + pick(0.0, inner_last.astype(jnp.float32))

    def part_outs(blocks):
        return [((half, width), jnp.float32 if block == 0 else jnp.bfloat16) for block in blocks]

    def forward(parts, experts, earlier=None):
        finish = experts[-1] == CORES - 1
        outs = part_outs(range(LINE)) if finish else [((line_rows, width), jnp.float32)]
        result = kernel_call(
            functools.partial(forward_kernel, owners, experts, experts[0] == 0, finish),
            "forward",
            where,
            parts,
            ([] if earlier is None else [earlier]) + [w for e in experts for w in weights[e]],
            outs + [((line_rows, hidden), jnp.float32)] * (2 * len(experts)),
            LINE,
            width,
            2 * 5 * line_rows * width * hidden * len(experts),
        )
        states = result[len(outs) :]
        return (result[: len(outs)] if finish else result[0]), states

    def backward(parts, states, experts, blocks=tuple(range(LINE)), earlier=None):
        start, finish = experts[0] == 0, experts[-1] == CORES - 1
        rows = len(blocks) * half
        outs = part_outs(blocks) if finish else [((rows, width), jnp.float32)]
        result = kernel_call(
            functools.partial(backward_kernel, experts, blocks, start, finish),
            "backward",
            where,
            parts,
            ([] if earlier is None else [earlier])
            + [s for e in experts for s in states[2 * e : 2 * e + 2]]
            + [w for e in experts for w in weights[e]],
            outs + ([((8, LANES), jnp.float32)] if start else []),
            len(blocks),
            width,
            2 * 3 * rows * width * hidden * len(experts),
        )
        squares = result[-1] if start else None
        return (result[: len(outs)] if finish else result[0]), squares

    pieces = gate_pieces(routes, gates, owners)
    halves = [slice(0, half), slice(half, token_count)]
    load_a, load_b = (
        jnp.concatenate([tokens[rows], tangent[rows], pieces[rows]], axis=1) for rows in halves
    )

    def slot(*results):
        return lax.optimization_barrier(results)

    def both_ways(part, payload):
        first = pick(part, payload[:, :width])
        if payload.shape[1] > width:
            first = jnp.concatenate([first, payload[:, width:]], axis=1)
        return side_hop(first)

    sib = [lax.ppermute(w, "expert", swap) for w in (w_gate, w_up, w_down)]
    a_side, a_near, own_weights, load_b = slot(
        side_hop(load_a), inner_hop(load_a), load((w_gate, w_up, w_down)), load_b
    )
    a_near_end, a_far, sib, load_b = slot(side_hop(a_near), inner_hop(a_side), sib, load_b)
    a_far_end, sib_weights, a_parts, load_b = slot(
        side_hop(a_far), load(sib), load((load_a, a_side, a_near, a_near_end, a_far)), load_b
    )
    weights = (own_weights, sib_weights)

    everyone = tuple(range(CORES))
    b_side, b_near, (pa, states_a) = slot(
        side_hop(load_b),
        inner_hop(load_b),
        forward((*a_parts, a_far_end), everyone),
    )
    b_near_end, b_far = slot(both_ways(pa[3], b_near), inner_hop(b_side))
    sa_far = add_rows(pa[3], b_near_end[:, :width])
    b_far_end, sa_side = slot(both_ways(pa[2], b_far), inner_hop(sa_far))
    sa_near = add_rows(pa[2], b_far_end[:, :width])
    b_parts = (load_b, b_side, b_near, b_near_end, b_far, b_far_end)
    came, last, (sum_b, states_b) = slot(
        both_ways(pa[1], add_rows(pa[1], sa_side)), inner_hop(sa_near), forward(b_parts, everyone[:1])
    )
    jv_a = tangent[:half].astype(jnp.float32) + home(pa, came, last)

    ja = jv_a.astype(jnp.bfloat16)
    side, near, (pb, rest_b) = slot(
        side_hop(ja), inner_hop(ja), forward(b_parts, everyone[1:], sum_b)
    )
    states_b = [*states_b, *rest_b]
    near_end, far = slot(both_ways(pb[3], near), inner_hop(side))
    s_far = add_rows(pb[3], near_end)
    far_end, s_side = slot(both_ways(pb[2], far), inner_hop(s_far))
    s_near = add_rows(pb[2], far_end)
    ja_parts = (ja, side, near, near_end, far, far_end)
    came, last, (sum_a, squares_a) = slot(
        both_ways(pb[1], add_rows(pb[1], s_side)),
        inner_hop(s_near),
        backward(ja_parts, states_a, everyone[:1]),
    )
    jv_b = tangent[half:].astype(jnp.float32) + home(pb, came, last)

    jb = jv_b.astype(jnp.bfloat16)
    side, near, (ga, _) = slot(
        side_hop(jb), inner_hop(jb), backward(ja_parts, states_a, everyone[1:], earlier=sum_a)
    )
    near_end, far = slot(both_ways(ga[3], near), inner_hop(side))
    s_far = add_rows(ga[3], near_end)
    far_end, s_side = slot(both_ways(ga[2], far), inner_hop(s_far))
    s_near = add_rows(ga[2], far_end)
    jb_parts = (jb, side, near, near_end, far, far_end)
    came, last, (gb, squares_b) = slot(
        both_ways(ga[1], add_rows(ga[1], s_side)),
        inner_hop(s_near),
        backward(jb_parts, states_b, everyone),
    )
    whole_a = jv_a + home(ga, came, last)

    lines = lax.axis_size("dp")
    squares = exchange_sum(squares_a + squares_b, "expert", 1)
    step = 1
    while step < lines // 2:
        squares = exchange_sum(squares, "dp", step)
        step *= 2
    came, squares = slot(side_hop(gb[3]), squares)
    came, s_side = slot(side_hop(gb[2]), inner_hop(add_rows(gb[3], came)))
    s_near = add_rows(gb[2], came)
    while step < lines:
        squares = exchange_sum(squares, "dp", step)
        step *= 2
    came, last = side_hop(pick(gb[1], add_rows(gb[1], s_side))), inner_hop(s_near)
    vmem = pl.BlockSpec(memory_space=pltpu.VMEM)
    return pl.pallas_call(
        functools.partial(output_kernel, token_count * width * lines * owners),
        in_specs=[pl.BlockSpec(memory_space=pltpu.SMEM)] + [vmem] * 6,
        out_specs=vmem,
        out_shape=jax.ShapeDtypeStruct((token_count, width), jnp.float32),
        compiler_params=pltpu.CompilerParams(vmem_limit_bytes=8 * 2**20),
        name="output",
    )(where, *[in_vmem(value) for value in (squares, whole_a, jv_b, gb[0], came, last)])


def owner_states(x_rows, gate_w, up_w):
    pre_a = dot(x_rows, gate_w)
    pre_b = dot(x_rows, up_w)
    sigma = jax.nn.sigmoid(pre_a)
    act = pre_a * sigma
    slope = sigma * (1.0 + pre_a * (1.0 - sigma))
    return (pre_b, act, slope)


def pair_shards(tokens, tangent, routes, gates, w_gate, w_up, w_down):
    token_count, model_width = tokens.shape
    top_k = routes.shape[1]
    owners = lax.axis_size("expert")
    expert_total = owners * w_gate.shape[0]
    capacity = pair_capacity(token_count, top_k, expert_total)
    slot_total = expert_total * capacity
    pair_count = token_count * top_k
    gate_w = w_gate[0]
    up_w = w_up[0]
    down_w = w_down[0]
    flat_routes = routes.reshape(pair_count)
    onehot = (flat_routes[:, None] == jnp.arange(expert_total, dtype=jnp.int32)[None, :]).astype(
        jnp.int32
    )
    before = jnp.cumsum(onehot, axis=0) - onehot
    slot_of = jnp.sum(before * onehot, axis=1)
    slot_index = flat_routes * capacity + slot_of
    slot_match = slot_index[None, :] == jnp.arange(slot_total, dtype=jnp.int32)[:, None]
    filled = jnp.any(slot_match, axis=1)
    pair_token = jnp.arange(pair_count, dtype=jnp.int32) // top_k
    source_token = jnp.sum(jnp.where(slot_match, pair_token[None, :], 0), axis=1)
    source_gate = jnp.sum(
        jnp.where(slot_match, gates.reshape(pair_count)[None, :], jnp.float32(0.0)), axis=1
    )
    keep_mask = filled.astype(jnp.bfloat16)[:, None]

    def exchange(rows):
        blocks = rows.reshape(owners, capacity, model_width)
        moved = lax.all_to_all(blocks, "expert", split_axis=0, concat_axis=0, tiled=True)
        return moved.reshape(slot_total, model_width)

    x_rows = exchange(jnp.take(tokens, source_token, axis=0) * keep_mask)
    v_rows = exchange(jnp.take(tangent, source_token, axis=0) * keep_mask)
    pre_b, act, slope = owner_states(x_rows, gate_w, up_w)
    tan_a = dot(v_rows, gate_w)
    tan_b = dot(v_rows, up_w)
    hidden_tangent = (slope * tan_a * pre_b + act * tan_b).astype(jnp.bfloat16)
    returned = exchange(dot(hidden_tangent, down_w).astype(jnp.bfloat16))
    picked_rows = jnp.take(returned, slot_index, axis=0)
    picked_rows = picked_rows.reshape(token_count, top_k, model_width)
    jv_vals = tangent.astype(jnp.float32) + jnp.sum(
        gates[:, :, None] * picked_rows.astype(jnp.float32), axis=1
    )
    cot_rows = exchange(
        (jnp.take(jv_vals, source_token, axis=0) * source_gate[:, None]).astype(jnp.bfloat16)
    )
    back_vals = dot_last(cot_rows, down_w)
    grad_gate = (back_vals * pre_b * slope).astype(jnp.bfloat16)
    grad_up = (back_vals * act).astype(jnp.bfloat16)
    pair_grad = dot_last(grad_gate, gate_w) + dot_last(grad_up, up_w)
    grad_rows = jnp.take(exchange(pair_grad.astype(jnp.bfloat16)), slot_index, axis=0)
    grad_rows = grad_rows.reshape(token_count, top_k, model_width)
    summed = jv_vals + jnp.sum(grad_rows.astype(jnp.float32), axis=1)
    global_sum = lax.psum(jnp.sum(jv_vals * jv_vals), ("dp", "expert"))
    element_count = token_count * lax.axis_size("dp") * owners * model_width
    return summed * lax.rsqrt(global_sum / element_count + 1e-06)


def pair_capacity(token_count, top_k, expert_total):
    return max(2, token_count * top_k * 9 // (8 * expert_total))


def shards(tokens, tangent, routes, gates, w_gate, w_up, w_down):
    token_count, top_k = routes.shape
    owners = lax.axis_size("expert")
    capacity = pair_capacity(token_count, top_k, owners * w_gate.shape[0])
    dp = lax.axis_size("dp")
    whole_blocks = (
        owners == CORES * LINE
        and dp & (dp - 1) == 0
        and w_gate.shape[0] == 1
        and token_count <= CORES * capacity
    )
    form = line_shards if whole_blocks else pair_shards
    return form(tokens, tangent, routes, gates, w_gate, w_up, w_down)


def solution(mesh):
    placed = (
        P(("dp", "expert"), None),
        P(("dp", "expert"), None),
        P(("dp", "expert"), None),
        P(("dp", "expert"), None),
        P("expert", None, None),
        P("expert", None, None),
        P("expert", None, None),
    )
    return jax.shard_map(
        shards, mesh=mesh, in_specs=placed, out_specs=P(("dp", "expert"), None), check_vma=False
    )
```

```python
import functools

import jax
import jax.numpy as jnp
from jax import lax
from jax.experimental import pallas as pl
from jax.experimental.pallas import tpu as pltpu
from jax.sharding import PartitionSpec as P

CONTRACT_LAST = (((1,), (1,)), ((), ()))


def dot(lhs, rhs):
    return jnp.dot(lhs, rhs, preferred_element_type=jnp.float32)


def dot_last(lhs, rhs):
    return lax.dot_general(lhs, rhs, CONTRACT_LAST, preferred_element_type=jnp.float32)


CORES, SIDES, ENDS = 2, 2, 2
LINE = SIDES * ENDS
SIDE_PAIRS = ((0, 1), (1, 0), (2, 3), (3, 2))
INNER_PAIRS = ((1, 2), (2, 1))


END_CHIPS = (0, 3)


def both_cores(pairs):
    return [(CORES * a + core, CORES * b + core) for a, b in pairs for core in range(CORES)]


def side_hop(rows):
    return lax.ppermute(rows, "expert", both_cores(SIDE_PAIRS))


def inner_hop(rows):
    idle = [(CORES * a + core, CORES * a + 1 - core) for a in END_CHIPS for core in range(CORES)]
    return lax.ppermute(rows, "expert", both_cores(INNER_PAIRS) + idle)


def add_rows(own, came):
    return (own.astype(jnp.float32) + came.astype(jnp.float32)).astype(jnp.bfloat16)


def in_vmem(value):
    return pltpu.with_memory_space_constraint(value, pltpu.VMEM)


LANES = 128
GATE_PIECES = 3


def fetch(inner, parts, blocks, out, sems):
    own, side, near, near_end, far, far_end = parts
    rows = own.shape[0]
    chosen = ((own, side, near, far), (own, side, near_end, far_end))

    def copies(mine):
        return [
            pltpu.make_async_copy(mine[block], out.at[pl.ds(i * rows, rows), :], sems.at[i])
            for i, block in enumerate(blocks)
        ]

    def begin(mine):
        for copy in copies(mine):
            copy.start()

    def finish(mine):
        for copy in copies(mine):
            copy.wait()

    for act in (begin, finish):
        pl.when(inner)(functools.partial(act, chosen[0]))
        pl.when(jnp.logical_not(inner))(functools.partial(act, chosen[1]))


def add_term(total, earlier, term):
    total[...] = term if earlier is None else earlier[...] + term


def store_parts(total, outs):
    for i, out in enumerate(outs):
        rows = out.shape[0]
        out[...] = total[pl.ds(i * rows, rows), :].astype(out.dtype)


def forward_kernel(owners, experts, start, finish, where_ref, *refs):
    refs = list(refs)
    parts, refs = refs[:6], refs[6:]
    earlier = None if start else refs.pop(0)
    weights, refs = refs[: 3 * len(experts)], refs[3 * len(experts) :]
    sems, load, total = refs[-3:]
    states = refs[-3 - 2 * len(experts) : -3]
    outs = refs[: -3 - 2 * len(experts)]
    if not finish:
        total = outs[0]
    width = total.shape[1]
    fetch(where_ref[0] == 1, parts, range(LINE), load, sems)
    x, v = load.at[:, pl.ds(0, width)], load.at[:, pl.ds(width, width)]
    gates = load.at[:, pl.ds(2 * width, LANES)]
    lane = lax.broadcasted_iota(jnp.int32, (1, LANES), 1)
    for i, which in enumerate(experts):
        gate_w, up_w, down_w = weights[3 * i : 3 * i + 3]
        expert = where_ref[1 + which]
        named = lane == expert
        for piece in range(1, GATE_PIECES):
            named = named | (lane == expert + piece * owners)
        g = jnp.sum(jnp.where(named, gates[...].astype(jnp.float32), 0.0), axis=1, keepdims=True)
        a, b = dot(x[...], gate_w[0]), dot(x[...], up_w[0])
        da, db = dot(v[...], gate_w[0]), dot(v[...], up_w[0])
        sigma = 1.0 / (1.0 + jnp.exp(-a))
        act = g * (a * sigma)
        b_slope = g * (sigma * (1.0 + a * (1.0 - sigma))) * b
        states[2 * i][...] = b_slope
        states[2 * i + 1][...] = act
        term = dot((b_slope * da + act * db).astype(jnp.bfloat16), down_w[0])
        add_term(total, earlier, term)
        earlier = total
    if finish:
        store_parts(total, outs)


def backward_kernel(experts, blocks, start, finish, where_ref, *refs):
    refs = list(refs)
    parts, refs = refs[:6], refs[6:]
    earlier = None if start else refs.pop(0)
    states, refs = refs[: 2 * len(experts)], refs[2 * len(experts) :]
    weights, refs = refs[: 3 * len(experts)], refs[3 * len(experts) :]
    sems, jv, total = refs[-3:]
    outs = refs[:-3]
    squares = outs.pop() if start else None
    if not finish:
        total = outs[0]
    rows = parts[0].shape[0]
    here = pl.ds(blocks[0] * rows, len(blocks) * rows)
    fetch(where_ref[0] == 1, parts, blocks, jv, sems)
    if start:
        sums = jnp.zeros((1, LANES), jnp.float32)
        for column in range(0, jv.shape[1], LANES):
            piece = jv[:, pl.ds(column, LANES)].astype(jnp.float32)
            sums = sums + jnp.sum(piece * piece, axis=0, keepdims=True)
        squares[...] = jnp.broadcast_to(sums, squares.shape)
    for i in range(len(experts)):
        gate_w, up_w, down_w = weights[3 * i : 3 * i + 3]
        back = dot_last(jv[...], down_w[0])
        grad_gate = (back * states[2 * i][here, :]).astype(jnp.bfloat16)
        grad_up = (back * states[2 * i + 1][here, :]).astype(jnp.bfloat16)
        term = dot_last(grad_gate, gate_w[0]) + dot_last(grad_up, up_w[0])
        add_term(total, earlier, term)
        earlier = total
    if finish:
        store_parts(total, outs)


def kernel_call(kernel, name, where, parts, operands, outs, blocks, width, flops):
    anywhere, vmem = pl.BlockSpec(memory_space=pl.ANY), pl.BlockSpec(memory_space=pltpu.VMEM)
    rows = parts[0].shape[0] * blocks
    return pl.pallas_call(
        kernel,
        in_specs=[pl.BlockSpec(memory_space=pltpu.SMEM)]
        + [anywhere] * len(parts)
        + [vmem] * len(operands),
        out_specs=[vmem] * len(outs),
        out_shape=[pltpu.VMEM(shape, kind) for shape, kind in outs],
        scratch_shapes=[
            pltpu.SemaphoreType.DMA((blocks,)),
            pltpu.VMEM((rows, parts[0].shape[1]), jnp.bfloat16),
            pltpu.VMEM((rows, width), jnp.float32),
        ],
        compiler_params=pltpu.CompilerParams(vmem_limit_bytes=10 * 2**20),
        cost_estimate=pl.CostEstimate(flops=flops, bytes_accessed=0, transcendentals=0),
        name=name,
    )(where, *parts, *[in_vmem(value) for value in operands])


def output_kernel(elements, where_ref, squares, whole_a, jv_b, own, side, inner_last, out):
    scale = lax.rsqrt(jnp.sum(squares[pl.ds(0, 1), :], axis=1, keepdims=True) / elements + 1e-06)
    half = whole_a.shape[0]
    out[pl.ds(0, half), :] = whole_a[...] * scale
    total = jv_b[...] + own[...] + side[...].astype(jnp.float32)
    inner = where_ref[0] == 1

    @pl.when(inner)
    def _():
        out[pl.ds(half, half), :] = (total + inner_last[...].astype(jnp.float32)) * scale

    @pl.when(jnp.logical_not(inner))
    def _():
        out[pl.ds(half, half), :] = total * scale


def load_kernel(count, *refs):
    arrays, outs, sems = refs[:count], refs[count : 2 * count], refs[2 * count]
    copies = [
        pltpu.make_async_copy(array, out, sems.at[i]) for i, (array, out) in enumerate(zip(arrays, outs))
    ]
    for copy in copies:
        copy.start()
    for copy in copies:
        copy.wait()


def load(arrays):
    return pl.pallas_call(
        functools.partial(load_kernel, len(arrays)),
        in_specs=[pl.BlockSpec(memory_space=pl.ANY)] * len(arrays),
        out_specs=[pl.BlockSpec(memory_space=pltpu.VMEM)] * len(arrays),
        out_shape=[pltpu.VMEM(array.shape, array.dtype) for array in arrays],
        scratch_shapes=[pltpu.SemaphoreType.DMA((len(arrays),))],
        compiler_params=pltpu.CompilerParams(vmem_limit_bytes=2**20),
        name="load",
    )(*arrays)


def exchange_sum(value, axis, step):
    pairs = [(i, i ^ step) for i in range(lax.axis_size(axis))]
    return value + lax.ppermute(value, axis, pairs)


def gate_pieces(routes, gates, owners):
    rest = jnp.sum(
        jnp.where(
            routes[:, :, None] == jnp.arange(owners, dtype=jnp.int32)[None, None, :],
            gates[:, :, None],
            jnp.float32(0.0),
        ),
        axis=1,
    )
    pieces = []
    for _ in range(GATE_PIECES):
        piece = lax.reduce_precision(rest, 8, 7)
        pieces.append(piece.astype(jnp.bfloat16))
        rest = rest - piece
    return jnp.pad(jnp.concatenate(pieces, axis=1), ((0, 0), (0, LANES - GATE_PIECES * owners)))


def line_shards(tokens, tangent, routes, gates, w_gate, w_up, w_down):
    token_count, width = tokens.shape
    hidden = w_gate.shape[2]
    owners = lax.axis_size("expert")
    me = lax.axis_index("expert")
    pos = me // CORES
    inner = (pos == 1) | (pos == 2)
    where = jnp.stack([inner.astype(jnp.int32), me, me ^ 1])
    half = token_count // 2
    line_rows = LINE * half
    swap = [(i, i ^ 1) for i in range(owners)]

    def pick(ends, inners):
        return jnp.where(inner, inners, ends)

    def home(parts, side, inner_last):
        return parts[0] + side.astype(jnp.float32) + pick(0.0, inner_last.astype(jnp.float32))

    def part_outs(blocks):
        return [((half, width), jnp.float32 if block == 0 else jnp.bfloat16) for block in blocks]

    def forward(parts, experts, earlier=None):
        finish = experts[-1] == CORES - 1
        outs = part_outs(range(LINE)) if finish else [((line_rows, width), jnp.float32)]
        result = kernel_call(
            functools.partial(forward_kernel, owners, experts, experts[0] == 0, finish),
            "forward",
            where,
            parts,
            ([] if earlier is None else [earlier]) + [w for e in experts for w in weights[e]],
            outs + [((line_rows, hidden), jnp.float32)] * (2 * len(experts)),
            LINE,
            width,
            2 * 5 * line_rows * width * hidden * len(experts),
        )
        states = result[len(outs) :]
        return (result[: len(outs)] if finish else result[0]), states

    def backward(parts, states, experts, blocks=tuple(range(LINE)), earlier=None):
        start, finish = experts[0] == 0, experts[-1] == CORES - 1
        rows = len(blocks) * half
        outs = part_outs(blocks) if finish else [((rows, width), jnp.float32)]
        result = kernel_call(
            functools.partial(backward_kernel, experts, blocks, start, finish),
            "backward",
            where,
            parts,
            ([] if earlier is None else [earlier])
            + [s for e in experts for s in states[2 * e : 2 * e + 2]]
            + [w for e in experts for w in weights[e]],
            outs + ([((8, LANES), jnp.float32)] if start else []),
            len(blocks),
            width,
            2 * 3 * rows * width * hidden * len(experts),
        )
        squares = result[-1] if start else None
        return (result[: len(outs)] if finish else result[0]), squares

    pieces = gate_pieces(routes, gates, owners)
    halves = [slice(0, half), slice(half, token_count)]
    load_a, load_b = (
        jnp.concatenate([tokens[rows], tangent[rows], pieces[rows]], axis=1) for rows in halves
    )

    def slot(*results):
        return lax.optimization_barrier(results)

    def both_ways(part, payload):
        first = pick(part, payload[:, :width])
        if payload.shape[1] > width:
            first = jnp.concatenate([first, payload[:, width:]], axis=1)
        return side_hop(first)

    sib = [lax.ppermute(w, "expert", swap) for w in (w_gate, w_up, w_down)]
    a_near, a_side, own_weights, load_b = slot(
        inner_hop(load_a), side_hop(load_a), load((w_gate, w_up, w_down)), load_b
    )
    a_far, a_near_end, sib, load_b = slot(inner_hop(a_side), side_hop(a_near), sib, load_b)
    a_far_end, sib_weights, a_parts, load_b = slot(
        side_hop(a_far), load(sib), load((load_a, a_side, a_near, a_near_end, a_far)), load_b
    )
    weights = (own_weights, sib_weights)

    everyone = tuple(range(CORES))
    b_near, b_side, (pa, states_a) = slot(
        inner_hop(load_b),
        side_hop(load_b),
        forward((*a_parts, a_far_end), everyone),
    )
    b_far, b_near_end = slot(inner_hop(b_side), both_ways(pa[3], b_near))
    sa_far = add_rows(pa[3], b_near_end[:, :width])
    sa_side, b_far_end = slot(inner_hop(sa_far), both_ways(pa[2], b_far))
    sa_near = add_rows(pa[2], b_far_end[:, :width])
    b_parts = (load_b, b_side, b_near, b_near_end, b_far, b_far_end)
    last, came, (sum_b, states_b) = slot(
        inner_hop(sa_near), both_ways(pa[1], add_rows(pa[1], sa_side)), forward(b_parts, everyone[:1])
    )
    jv_a = tangent[:half].astype(jnp.float32) + home(pa, came, last)

    ja = jv_a.astype(jnp.bfloat16)
    near, side, (pb, rest_b) = slot(
        inner_hop(ja), side_hop(ja), forward(b_parts, everyone[1:], sum_b)
    )
    states_b = [*states_b, *rest_b]
    far, near_end = slot(inner_hop(side), both_ways(pb[3], near))
    s_far = add_rows(pb[3], near_end)
    s_side, far_end = slot(inner_hop(s_far), both_ways(pb[2], far))
    s_near = add_rows(pb[2], far_end)
    ja_parts = (ja, side, near, near_end, far, far_end)
    last, came, (sum_a, squares_a) = slot(
        inner_hop(s_near),
        both_ways(pb[1], add_rows(pb[1], s_side)),
        backward(ja_parts, states_a, everyone[:1]),
    )
    jv_b = tangent[half:].astype(jnp.float32) + home(pb, came, last)

    jb = jv_b.astype(jnp.bfloat16)
    near, side, (ga, _) = slot(
        inner_hop(jb), side_hop(jb), backward(ja_parts, states_a, everyone[1:], earlier=sum_a)
    )
    far, near_end = slot(inner_hop(side), both_ways(ga[3], near))
    s_far = add_rows(ga[3], near_end)
    s_side, far_end = slot(inner_hop(s_far), both_ways(ga[2], far))
    s_near = add_rows(ga[2], far_end)
    jb_parts = (jb, side, near, near_end, far, far_end)
    last, came, (gb, squares_b) = slot(
        inner_hop(s_near),
        both_ways(ga[1], add_rows(ga[1], s_side)),
        backward(jb_parts, states_b, everyone),
    )
    whole_a = jv_a + home(ga, came, last)

    lines = lax.axis_size("dp")
    squares = exchange_sum(squares_a + squares_b, "expert", 1)
    step = 1
    while step < lines // 2:
        squares = exchange_sum(squares, "dp", step)
        step *= 2
    came, squares = slot(side_hop(gb[3]), squares)
    s_side, came = slot(inner_hop(add_rows(gb[3], came)), side_hop(gb[2]))
    s_near = add_rows(gb[2], came)
    while step < lines:
        squares = exchange_sum(squares, "dp", step)
        step *= 2
    came, last = side_hop(pick(gb[1], add_rows(gb[1], s_side))), inner_hop(s_near)
    vmem = pl.BlockSpec(memory_space=pltpu.VMEM)
    return pl.pallas_call(
        functools.partial(output_kernel, token_count * width * lines * owners),
        in_specs=[pl.BlockSpec(memory_space=pltpu.SMEM)] + [vmem] * 6,
        out_specs=vmem,
        out_shape=jax.ShapeDtypeStruct((token_count, width), jnp.float32),
        compiler_params=pltpu.CompilerParams(vmem_limit_bytes=8 * 2**20),
        name="output",
    )(where, *[in_vmem(value) for value in (squares, whole_a, jv_b, gb[0], came, last)])


def owner_states(x_rows, gate_w, up_w):
    pre_a = dot(x_rows, gate_w)
    pre_b = dot(x_rows, up_w)
    sigma = jax.nn.sigmoid(pre_a)
    act = pre_a * sigma
    slope = sigma * (1.0 + pre_a * (1.0 - sigma))
    return (pre_b, act, slope)


def pair_shards(tokens, tangent, routes, gates, w_gate, w_up, w_down):
    token_count, model_width = tokens.shape
    top_k = routes.shape[1]
    owners = lax.axis_size("expert")
    expert_total = owners * w_gate.shape[0]
    capacity = pair_capacity(token_count, top_k, expert_total)
    slot_total = expert_total * capacity
    pair_count = token_count * top_k
    gate_w = w_gate[0]
    up_w = w_up[0]
    down_w = w_down[0]
    flat_routes = routes.reshape(pair_count)
    onehot = (flat_routes[:, None] == jnp.arange(expert_total, dtype=jnp.int32)[None, :]).astype(
        jnp.int32
    )
    before = jnp.cumsum(onehot, axis=0) - onehot
    slot_of = jnp.sum(before * onehot, axis=1)
    slot_index = flat_routes * capacity + slot_of
    slot_match = slot_index[None, :] == jnp.arange(slot_total, dtype=jnp.int32)[:, None]
    filled = jnp.any(slot_match, axis=1)
    pair_token = jnp.arange(pair_count, dtype=jnp.int32) // top_k
    source_token = jnp.sum(jnp.where(slot_match, pair_token[None, :], 0), axis=1)
    source_gate = jnp.sum(
        jnp.where(slot_match, gates.reshape(pair_count)[None, :], jnp.float32(0.0)), axis=1
    )
    keep_mask = filled.astype(jnp.bfloat16)[:, None]

    def exchange(rows):
        blocks = rows.reshape(owners, capacity, model_width)
        moved = lax.all_to_all(blocks, "expert", split_axis=0, concat_axis=0, tiled=True)
        return moved.reshape(slot_total, model_width)

    x_rows = exchange(jnp.take(tokens, source_token, axis=0) * keep_mask)
    v_rows = exchange(jnp.take(tangent, source_token, axis=0) * keep_mask)
    pre_b, act, slope = owner_states(x_rows, gate_w, up_w)
    tan_a = dot(v_rows, gate_w)
    tan_b = dot(v_rows, up_w)
    hidden_tangent = (slope * tan_a * pre_b + act * tan_b).astype(jnp.bfloat16)
    returned = exchange(dot(hidden_tangent, down_w).astype(jnp.bfloat16))
    picked_rows = jnp.take(returned, slot_index, axis=0)
    picked_rows = picked_rows.reshape(token_count, top_k, model_width)
    jv_vals = tangent.astype(jnp.float32) + jnp.sum(
        gates[:, :, None] * picked_rows.astype(jnp.float32), axis=1
    )
    cot_rows = exchange(
        (jnp.take(jv_vals, source_token, axis=0) * source_gate[:, None]).astype(jnp.bfloat16)
    )
    back_vals = dot_last(cot_rows, down_w)
    grad_gate = (back_vals * pre_b * slope).astype(jnp.bfloat16)
    grad_up = (back_vals * act).astype(jnp.bfloat16)
    pair_grad = dot_last(grad_gate, gate_w) + dot_last(grad_up, up_w)
    grad_rows = jnp.take(exchange(pair_grad.astype(jnp.bfloat16)), slot_index, axis=0)
    grad_rows = grad_rows.reshape(token_count, top_k, model_width)
    summed = jv_vals + jnp.sum(grad_rows.astype(jnp.float32), axis=1)
    global_sum = lax.psum(jnp.sum(jv_vals * jv_vals), ("dp", "expert"))
    element_count = token_count * lax.axis_size("dp") * owners * model_width
    return summed * lax.rsqrt(global_sum / element_count + 1e-06)


def pair_capacity(token_count, top_k, expert_total):
    return max(2, token_count * top_k * 9 // (8 * expert_total))


def shards(tokens, tangent, routes, gates, w_gate, w_up, w_down):
    token_count, top_k = routes.shape
    owners = lax.axis_size("expert")
    capacity = pair_capacity(token_count, top_k, owners * w_gate.shape[0])
    dp = lax.axis_size("dp")
    whole_blocks = (
        owners == CORES * LINE
        and dp & (dp - 1) == 0
        and w_gate.shape[0] == 1
        and token_count <= CORES * capacity
    )
    form = line_shards if whole_blocks else pair_shards
    return form(tokens, tangent, routes, gates, w_gate, w_up, w_down)


def solution(mesh):
    placed = (
        P(("dp", "expert"), None),
        P(("dp", "expert"), None),
        P(("dp", "expert"), None),
        P(("dp", "expert"), None),
        P("expert", None, None),
        P("expert", None, None),
        P("expert", None, None),
    )
    return jax.shard_map(
        shards, mesh=mesh, in_specs=placed, out_specs=P(("dp", "expert"), None), check_vma=False
    )
```

```python
import functools

import jax
import jax.numpy as jnp
from jax import lax
from jax.experimental import pallas as pl
from jax.experimental.pallas import tpu as pltpu
from jax.sharding import PartitionSpec as P

CONTRACT_LAST = (((1,), (1,)), ((), ()))


def dot(lhs, rhs):
    return jnp.dot(lhs, rhs, preferred_element_type=jnp.float32)


def dot_last(lhs, rhs):
    return lax.dot_general(lhs, rhs, CONTRACT_LAST, preferred_element_type=jnp.float32)


CORES, SIDES, ENDS = 2, 2, 2
LINE = SIDES * ENDS
SIDE_PAIRS = ((0, 1), (1, 0), (2, 3), (3, 2))
INNER_PAIRS = ((1, 2), (2, 1))


END_CHIPS = (0, 3)


def both_cores(pairs):
    return [(CORES * a + core, CORES * b + core) for a, b in pairs for core in range(CORES)]


def side_hop(rows):
    return lax.ppermute(rows, "expert", both_cores(SIDE_PAIRS))


def inner_hop(rows):
    idle = [(CORES * a + core, CORES * a + 1 - core) for a in END_CHIPS for core in range(CORES)]
    return lax.ppermute(rows, "expert", both_cores(INNER_PAIRS) + idle)


def add_rows(own, came):
    return (own.astype(jnp.float32) + came.astype(jnp.float32)).astype(jnp.bfloat16)


def in_vmem(value):
    return pltpu.with_memory_space_constraint(value, pltpu.VMEM)


LANES = 128
GATE_PIECES = 3


def fetch(inner, parts, blocks, out, sems):
    own, side, near, near_end, far, far_end = parts
    rows = own.shape[0]
    chosen = ((own, side, near, far), (own, side, near_end, far_end))

    def copies(mine):
        return [
            pltpu.make_async_copy(mine[block], out.at[pl.ds(i * rows, rows), :], sems.at[i])
            for i, block in enumerate(blocks)
        ]

    def begin(mine):
        for copy in copies(mine):
            copy.start()

    def finish(mine):
        for copy in copies(mine):
            copy.wait()

    for act in (begin, finish):
        pl.when(inner)(functools.partial(act, chosen[0]))
        pl.when(jnp.logical_not(inner))(functools.partial(act, chosen[1]))


def add_term(total, earlier, term):
    total[...] = term if earlier is None else earlier[...] + term


def store_parts(total, outs):
    for i, out in enumerate(outs):
        rows = out.shape[0]
        out[...] = total[pl.ds(i * rows, rows), :].astype(out.dtype)


def forward_kernel(owners, experts, start, finish, where_ref, *refs):
    refs = list(refs)
    parts, refs = refs[:6], refs[6:]
    earlier = None if start else refs.pop(0)
    weights, refs = refs[: 3 * len(experts)], refs[3 * len(experts) :]
    sems, load, total = refs[-3:]
    states = refs[-3 - 2 * len(experts) : -3]
    outs = refs[: -3 - 2 * len(experts)]
    if not finish:
        total = outs[0]
    width = total.shape[1]
    fetch(where_ref[0] == 1, parts, range(LINE), load, sems)
    x, v = load.at[:, pl.ds(0, width)], load.at[:, pl.ds(width, width)]
    gates = load.at[:, pl.ds(2 * width, LANES)]
    lane = lax.broadcasted_iota(jnp.int32, (1, LANES), 1)
    for i, which in enumerate(experts):
        gate_w, up_w, down_w = weights[3 * i : 3 * i + 3]
        expert = where_ref[1 + which]
        named = lane == expert
        for piece in range(1, GATE_PIECES):
            named = named | (lane == expert + piece * owners)
        g = jnp.sum(jnp.where(named, gates[...].astype(jnp.float32), 0.0), axis=1, keepdims=True)
        a, b = dot(x[...], gate_w[0]), dot(x[...], up_w[0])
        da, db = dot(v[...], gate_w[0]), dot(v[...], up_w[0])
        sigma = 1.0 / (1.0 + jnp.exp(-a))
        act = g * (a * sigma)
        b_slope = g * (sigma * (1.0 + a * (1.0 - sigma))) * b
        states[2 * i][...] = b_slope
        states[2 * i + 1][...] = act
        term = dot((b_slope * da + act * db).astype(jnp.bfloat16), down_w[0])
        add_term(total, earlier, term)
        earlier = total
    if finish:
        store_parts(total, outs)


def backward_kernel(experts, blocks, start, finish, where_ref, *refs):
    refs = list(refs)
    parts, refs = refs[:6], refs[6:]
    earlier = None if start else refs.pop(0)
    states, refs = refs[: 2 * len(experts)], refs[2 * len(experts) :]
    weights, refs = refs[: 3 * len(experts)], refs[3 * len(experts) :]
    sems, jv, total = refs[-3:]
    outs = refs[:-3]
    squares = outs.pop() if start else None
    if not finish:
        total = outs[0]
    rows = parts[0].shape[0]
    here = pl.ds(blocks[0] * rows, len(blocks) * rows)
    fetch(where_ref[0] == 1, parts, blocks, jv, sems)
    if start:
        sums = jnp.zeros((1, LANES), jnp.float32)
        for column in range(0, jv.shape[1], LANES):
            piece = jv[:, pl.ds(column, LANES)].astype(jnp.float32)
            sums = sums + jnp.sum(piece * piece, axis=0, keepdims=True)
        squares[...] = jnp.broadcast_to(sums, squares.shape)
    for i in range(len(experts)):
        gate_w, up_w, down_w = weights[3 * i : 3 * i + 3]
        back = dot_last(jv[...], down_w[0])
        grad_gate = (back * states[2 * i][here, :]).astype(jnp.bfloat16)
        grad_up = (back * states[2 * i + 1][here, :]).astype(jnp.bfloat16)
        term = dot_last(grad_gate, gate_w[0]) + dot_last(grad_up, up_w[0])
        add_term(total, earlier, term)
        earlier = total
    if finish:
        store_parts(total, outs)


def kernel_call(kernel, name, where, parts, operands, outs, blocks, width, flops):
    anywhere, vmem = pl.BlockSpec(memory_space=pl.ANY), pl.BlockSpec(memory_space=pltpu.VMEM)
    rows = parts[0].shape[0] * blocks
    return pl.pallas_call(
        kernel,
        in_specs=[pl.BlockSpec(memory_space=pltpu.SMEM)]
        + [anywhere] * len(parts)
        + [vmem] * len(operands),
        out_specs=[vmem] * len(outs),
        out_shape=[pltpu.VMEM(shape, kind) for shape, kind in outs],
        scratch_shapes=[
            pltpu.SemaphoreType.DMA((blocks,)),
            pltpu.VMEM((rows, parts[0].shape[1]), jnp.bfloat16),
            pltpu.VMEM((rows, width), jnp.float32),
        ],
        compiler_params=pltpu.CompilerParams(vmem_limit_bytes=10 * 2**20),
        cost_estimate=pl.CostEstimate(flops=flops, bytes_accessed=0, transcendentals=0),
        name=name,
    )(where, *parts, *[in_vmem(value) for value in operands])


def output_kernel(elements, where_ref, squares, whole_a, jv_b, own, side, inner_last, out):
    scale = lax.rsqrt(jnp.sum(squares[pl.ds(0, 1), :], axis=1, keepdims=True) / elements + 1e-06)
    half = whole_a.shape[0]
    out[pl.ds(0, half), :] = whole_a[...] * scale
    total = jv_b[...] + own[...] + side[...].astype(jnp.float32)
    inner = where_ref[0] == 1

    @pl.when(inner)
    def _():
        out[pl.ds(half, half), :] = (total + inner_last[...].astype(jnp.float32)) * scale

    @pl.when(jnp.logical_not(inner))
    def _():
        out[pl.ds(half, half), :] = total * scale


def load_kernel(count, *refs):
    arrays, outs, sems = refs[:count], refs[count : 2 * count], refs[2 * count]
    copies = [
        pltpu.make_async_copy(array, out, sems.at[i]) for i, (array, out) in enumerate(zip(arrays, outs))
    ]
    for copy in copies:
        copy.start()
    for copy in copies:
        copy.wait()


def load(arrays):
    return pl.pallas_call(
        functools.partial(load_kernel, len(arrays)),
        in_specs=[pl.BlockSpec(memory_space=pl.ANY)] * len(arrays),
        out_specs=[pl.BlockSpec(memory_space=pltpu.VMEM)] * len(arrays),
        out_shape=[pltpu.VMEM(array.shape, array.dtype) for array in arrays],
        scratch_shapes=[pltpu.SemaphoreType.DMA((len(arrays),))],
        compiler_params=pltpu.CompilerParams(vmem_limit_bytes=2**20),
        name="load",
    )(*arrays)


def exchange_sum(value, axis, step):
    pairs = [(i, i ^ step) for i in range(lax.axis_size(axis))]
    return value + lax.ppermute(value, axis, pairs)


def gate_pieces(routes, gates, owners):
    rest = jnp.sum(
        jnp.where(
            routes[:, :, None] == jnp.arange(owners, dtype=jnp.int32)[None, None, :],
            gates[:, :, None],
            jnp.float32(0.0),
        ),
        axis=1,
    )
    pieces = []
    for _ in range(GATE_PIECES):
        piece = lax.reduce_precision(rest, 8, 7)
        pieces.append(piece.astype(jnp.bfloat16))
        rest = rest - piece
    return jnp.pad(jnp.concatenate(pieces, axis=1), ((0, 0), (0, LANES - GATE_PIECES * owners)))


def line_shards(tokens, tangent, routes, gates, w_gate, w_up, w_down):
    token_count, width = tokens.shape
    hidden = w_gate.shape[2]
    owners = lax.axis_size("expert")
    me = lax.axis_index("expert")
    pos = me // CORES
    inner = (pos == 1) | (pos == 2)
    where = jnp.stack([inner.astype(jnp.int32), me, me ^ 1])
    half = token_count // 2
    line_rows = LINE * half
    swap = [(i, i ^ 1) for i in range(owners)]

    def pick(ends, inners):
        return jnp.where(inner, inners, ends)

    def home(parts, side, inner_last):
        return parts[0] + side.astype(jnp.float32) + pick(0.0, inner_last.astype(jnp.float32))

    def part_outs(blocks):
        return [((half, width), jnp.float32 if block == 0 else jnp.bfloat16) for block in blocks]

    def forward(parts, experts, earlier=None):
        finish = experts[-1] == CORES - 1
        outs = part_outs(range(LINE)) if finish else [((line_rows, width), jnp.float32)]
        result = kernel_call(
            functools.partial(forward_kernel, owners, experts, experts[0] == 0, finish),
            "forward",
            where,
            parts,
            ([] if earlier is None else [earlier]) + [w for e in experts for w in weights[e]],
            outs + [((line_rows, hidden), jnp.float32)] * (2 * len(experts)),
            LINE,
            width,
            2 * 5 * line_rows * width * hidden * len(experts),
        )
        states = result[len(outs) :]
        return (result[: len(outs)] if finish else result[0]), states

    def backward(parts, states, experts, blocks=tuple(range(LINE)), earlier=None):
        start, finish = experts[0] == 0, experts[-1] == CORES - 1
        rows = len(blocks) * half
        outs = part_outs(blocks) if finish else [((rows, width), jnp.float32)]
        result = kernel_call(
            functools.partial(backward_kernel, experts, blocks, start, finish),
            "backward",
            where,
            parts,
            ([] if earlier is None else [earlier])
            + [s for e in experts for s in states[2 * e : 2 * e + 2]]
            + [w for e in experts for w in weights[e]],
            outs + ([((8, LANES), jnp.float32)] if start else []),
            len(blocks),
            width,
            2 * 3 * rows * width * hidden * len(experts),
        )
        squares = result[-1] if start else None
        return (result[: len(outs)] if finish else result[0]), squares

    pieces = gate_pieces(routes, gates, owners)
    halves = [slice(0, half), slice(half, token_count)]
    load_a, load_b = (
        jnp.concatenate([tokens[rows], tangent[rows], pieces[rows]], axis=1) for rows in halves
    )

    def slot(*results):
        return lax.optimization_barrier(results)

    def both_ways(part, payload):
        first = pick(part, payload[:, :width])
        if payload.shape[1] > width:
            first = jnp.concatenate([first, payload[:, width:]], axis=1)
        return side_hop(first)

    sib = [lax.ppermute(w, "expert", swap) for w in (w_gate, w_up, w_down)]
    a_near, a_side, own_weights, load_b = slot(
        inner_hop(load_a), side_hop(load_a), load((w_gate, w_up, w_down)), load_b
    )
    a_near_end, a_far, sib, first_parts, load_b = slot(
        side_hop(a_near), inner_hop(a_side), sib, load((load_a, a_side, a_near)), load_b
    )
    a_far_end, sib_weights, more_parts, load_b = slot(
        side_hop(a_far), load(sib), load((a_near_end, a_far)), load_b
    )
    a_parts = (*first_parts, *more_parts)
    weights = (own_weights, sib_weights)

    everyone = tuple(range(CORES))
    b_near, b_side, (pa, states_a) = slot(
        inner_hop(load_b),
        side_hop(load_b),
        forward((*a_parts, a_far_end), everyone),
    )
    b_far, b_near_end = slot(inner_hop(b_side), both_ways(pa[3], b_near))
    sa_far = add_rows(pa[3], b_near_end[:, :width])
    sa_side, b_far_end = slot(inner_hop(sa_far), both_ways(pa[2], b_far))
    sa_near = add_rows(pa[2], b_far_end[:, :width])
    b_parts = (load_b, b_side, b_near, b_near_end, b_far, b_far_end)
    last, came, (sum_b, states_b) = slot(
        inner_hop(sa_near), both_ways(pa[1], add_rows(pa[1], sa_side)), forward(b_parts, everyone[:1])
    )
    jv_a = tangent[:half].astype(jnp.float32) + home(pa, came, last)

    ja = jv_a.astype(jnp.bfloat16)
    near, side, (pb, rest_b) = slot(
        inner_hop(ja), side_hop(ja), forward(b_parts, everyone[1:], sum_b)
    )
    states_b = [*states_b, *rest_b]
    far, near_end = slot(inner_hop(side), both_ways(pb[3], near))
    s_far = add_rows(pb[3], near_end)
    s_side, far_end = slot(inner_hop(s_far), both_ways(pb[2], far))
    s_near = add_rows(pb[2], far_end)
    ja_parts = (ja, side, near, near_end, far, far_end)
    last, came, (sum_a, squares_a) = slot(
        inner_hop(s_near),
        both_ways(pb[1], add_rows(pb[1], s_side)),
        backward(ja_parts, states_a, everyone[:1]),
    )
    jv_b = tangent[half:].astype(jnp.float32) + home(pb, came, last)

    jb = jv_b.astype(jnp.bfloat16)
    near, side, (ga, _) = slot(
        inner_hop(jb), side_hop(jb), backward(ja_parts, states_a, everyone[1:], earlier=sum_a)
    )
    far, near_end = slot(inner_hop(side), both_ways(ga[3], near))
    s_far = add_rows(ga[3], near_end)
    s_side, far_end = slot(inner_hop(s_far), both_ways(ga[2], far))
    s_near = add_rows(ga[2], far_end)
    jb_parts = (jb, side, near, near_end, far, far_end)
    last, came, (gb, squares_b) = slot(
        inner_hop(s_near),
        both_ways(ga[1], add_rows(ga[1], s_side)),
        backward(jb_parts, states_b, everyone),
    )
    whole_a = jv_a + home(ga, came, last)

    lines = lax.axis_size("dp")
    squares = exchange_sum(squares_a + squares_b, "expert", 1)
    step = 1
    while step < lines // 2:
        squares = exchange_sum(squares, "dp", step)
        step *= 2
    came, squares = slot(side_hop(gb[3]), squares)
    s_side, came = slot(inner_hop(add_rows(gb[3], came)), side_hop(gb[2]))
    s_near = add_rows(gb[2], came)
    while step < lines:
        squares = exchange_sum(squares, "dp", step)
        step *= 2
    last, came = slot(inner_hop(s_near), side_hop(pick(gb[1], add_rows(gb[1], s_side))))
    vmem = pl.BlockSpec(memory_space=pltpu.VMEM)
    return pl.pallas_call(
        functools.partial(output_kernel, token_count * width * lines * owners),
        in_specs=[pl.BlockSpec(memory_space=pltpu.SMEM)] + [vmem] * 6,
        out_specs=vmem,
        out_shape=jax.ShapeDtypeStruct((token_count, width), jnp.float32),
        compiler_params=pltpu.CompilerParams(vmem_limit_bytes=8 * 2**20),
        name="output",
    )(where, *[in_vmem(value) for value in (squares, whole_a, jv_b, gb[0], came, last)])


def owner_states(x_rows, gate_w, up_w):
    pre_a = dot(x_rows, gate_w)
    pre_b = dot(x_rows, up_w)
    sigma = jax.nn.sigmoid(pre_a)
    act = pre_a * sigma
    slope = sigma * (1.0 + pre_a * (1.0 - sigma))
    return (pre_b, act, slope)


def pair_shards(tokens, tangent, routes, gates, w_gate, w_up, w_down):
    token_count, model_width = tokens.shape
    top_k = routes.shape[1]
    owners = lax.axis_size("expert")
    expert_total = owners * w_gate.shape[0]
    capacity = pair_capacity(token_count, top_k, expert_total)
    slot_total = expert_total * capacity
    pair_count = token_count * top_k
    gate_w = w_gate[0]
    up_w = w_up[0]
    down_w = w_down[0]
    flat_routes = routes.reshape(pair_count)
    onehot = (flat_routes[:, None] == jnp.arange(expert_total, dtype=jnp.int32)[None, :]).astype(
        jnp.int32
    )
    before = jnp.cumsum(onehot, axis=0) - onehot
    slot_of = jnp.sum(before * onehot, axis=1)
    slot_index = flat_routes * capacity + slot_of
    slot_match = slot_index[None, :] == jnp.arange(slot_total, dtype=jnp.int32)[:, None]
    filled = jnp.any(slot_match, axis=1)
    pair_token = jnp.arange(pair_count, dtype=jnp.int32) // top_k
    source_token = jnp.sum(jnp.where(slot_match, pair_token[None, :], 0), axis=1)
    source_gate = jnp.sum(
        jnp.where(slot_match, gates.reshape(pair_count)[None, :], jnp.float32(0.0)), axis=1
    )
    keep_mask = filled.astype(jnp.bfloat16)[:, None]

    def exchange(rows):
        blocks = rows.reshape(owners, capacity, model_width)
        moved = lax.all_to_all(blocks, "expert", split_axis=0, concat_axis=0, tiled=True)
        return moved.reshape(slot_total, model_width)

    x_rows = exchange(jnp.take(tokens, source_token, axis=0) * keep_mask)
    v_rows = exchange(jnp.take(tangent, source_token, axis=0) * keep_mask)
    pre_b, act, slope = owner_states(x_rows, gate_w, up_w)
    tan_a = dot(v_rows, gate_w)
    tan_b = dot(v_rows, up_w)
    hidden_tangent = (slope * tan_a * pre_b + act * tan_b).astype(jnp.bfloat16)
    returned = exchange(dot(hidden_tangent, down_w).astype(jnp.bfloat16))
    picked_rows = jnp.take(returned, slot_index, axis=0)
    picked_rows = picked_rows.reshape(token_count, top_k, model_width)
    jv_vals = tangent.astype(jnp.float32) + jnp.sum(
        gates[:, :, None] * picked_rows.astype(jnp.float32), axis=1
    )
    cot_rows = exchange(
        (jnp.take(jv_vals, source_token, axis=0) * source_gate[:, None]).astype(jnp.bfloat16)
    )
    back_vals = dot_last(cot_rows, down_w)
    grad_gate = (back_vals * pre_b * slope).astype(jnp.bfloat16)
    grad_up = (back_vals * act).astype(jnp.bfloat16)
    pair_grad = dot_last(grad_gate, gate_w) + dot_last(grad_up, up_w)
    grad_rows = jnp.take(exchange(pair_grad.astype(jnp.bfloat16)), slot_index, axis=0)
    grad_rows = grad_rows.reshape(token_count, top_k, model_width)
    summed = jv_vals + jnp.sum(grad_rows.astype(jnp.float32), axis=1)
    global_sum = lax.psum(jnp.sum(jv_vals * jv_vals), ("dp", "expert"))
    element_count = token_count * lax.axis_size("dp") * owners * model_width
    return summed * lax.rsqrt(global_sum / element_count + 1e-06)


def pair_capacity(token_count, top_k, expert_total):
    return max(2, token_count * top_k * 9 // (8 * expert_total))


def shards(tokens, tangent, routes, gates, w_gate, w_up, w_down):
    token_count, top_k = routes.shape
    owners = lax.axis_size("expert")
    capacity = pair_capacity(token_count, top_k, owners * w_gate.shape[0])
    dp = lax.axis_size("dp")
    whole_blocks = (
        owners == CORES * LINE
        and dp & (dp - 1) == 0
        and w_gate.shape[0] == 1
        and token_count <= CORES * capacity
    )
    form = line_shards if whole_blocks else pair_shards
    return form(tokens, tangent, routes, gates, w_gate, w_up, w_down)


def solution(mesh):
    placed = (
        P(("dp", "expert"), None),
        P(("dp", "expert"), None),
        P(("dp", "expert"), None),
        P(("dp", "expert"), None),
        P("expert", None, None),
        P("expert", None, None),
        P("expert", None, None),
    )
    return jax.shard_map(
        shards, mesh=mesh, in_specs=placed, out_specs=P(("dp", "expert"), None), check_vma=False
    )
```

```python
import functools

import jax
import jax.numpy as jnp
from jax import lax
from jax.experimental import pallas as pl
from jax.experimental.pallas import tpu as pltpu
from jax.sharding import PartitionSpec as P

CONTRACT_LAST = (((1,), (1,)), ((), ()))


def dot(lhs, rhs):
    return jnp.dot(lhs, rhs, preferred_element_type=jnp.float32)


def dot_last(lhs, rhs):
    return lax.dot_general(lhs, rhs, CONTRACT_LAST, preferred_element_type=jnp.float32)


CORES, SIDES, ENDS = 2, 2, 2
LINE = SIDES * ENDS
SIDE_PAIRS = ((0, 1), (1, 0), (2, 3), (3, 2))
INNER_PAIRS = ((1, 2), (2, 1))


END_CHIPS = (0, 3)


def both_cores(pairs):
    return [(CORES * a + core, CORES * b + core) for a, b in pairs for core in range(CORES)]


def side_hop(rows):
    return lax.ppermute(rows, "expert", both_cores(SIDE_PAIRS))


def inner_hop(rows):
    idle = [(CORES * a + core, CORES * a + 1 - core) for a in END_CHIPS for core in range(CORES)]
    return lax.ppermute(rows, "expert", both_cores(INNER_PAIRS) + idle)


def add_rows(own, came):
    return (own.astype(jnp.float32) + came.astype(jnp.float32)).astype(jnp.bfloat16)


def in_vmem(value):
    return pltpu.with_memory_space_constraint(value, pltpu.VMEM)


LANES = 128
GATE_PIECES = 3


def fetch(inner, parts, blocks, out, sems):
    own, side, near, near_end, far, far_end = parts
    rows = own.shape[0]
    chosen = ((own, side, near, far), (own, side, near_end, far_end))

    def copies(mine):
        return [
            pltpu.make_async_copy(mine[block], out.at[pl.ds(i * rows, rows), :], sems.at[i])
            for i, block in enumerate(blocks)
        ]

    def begin(mine):
        for copy in copies(mine):
            copy.start()

    def finish(mine):
        for copy in copies(mine):
            copy.wait()

    for act in (begin, finish):
        pl.when(inner)(functools.partial(act, chosen[0]))
        pl.when(jnp.logical_not(inner))(functools.partial(act, chosen[1]))


def add_term(total, earlier, term):
    total[...] = term if earlier is None else earlier[...] + term


def store_parts(total, outs):
    for i, out in enumerate(outs):
        rows = out.shape[0]
        out[...] = total[pl.ds(i * rows, rows), :].astype(out.dtype)


def forward_kernel(owners, experts, start, finish, where_ref, *refs):
    refs = list(refs)
    parts, refs = refs[:6], refs[6:]
    earlier = None if start else refs.pop(0)
    weights, refs = refs[: 3 * len(experts)], refs[3 * len(experts) :]
    sems, load, total = refs[-3:]
    states = refs[-3 - 2 * len(experts) : -3]
    outs = refs[: -3 - 2 * len(experts)]
    if not finish:
        total = outs[0]
    width = total.shape[1]
    fetch(where_ref[0] == 1, parts, range(LINE), load, sems)
    x, v = load.at[:, pl.ds(0, width)], load.at[:, pl.ds(width, width)]
    gates = load.at[:, pl.ds(2 * width, LANES)]
    lane = lax.broadcasted_iota(jnp.int32, (1, LANES), 1)
    for i, which in enumerate(experts):
        gate_w, up_w, down_w = weights[3 * i : 3 * i + 3]
        expert = where_ref[1 + which]
        named = lane == expert
        for piece in range(1, GATE_PIECES):
            named = named | (lane == expert + piece * owners)
        g = jnp.sum(jnp.where(named, gates[...].astype(jnp.float32), 0.0), axis=1, keepdims=True)
        a, b = dot(x[...], gate_w[0]), dot(x[...], up_w[0])
        da, db = dot(v[...], gate_w[0]), dot(v[...], up_w[0])
        sigma = 1.0 / (1.0 + jnp.exp(-a))
        act = g * (a * sigma)
        b_slope = g * (sigma * (1.0 + a * (1.0 - sigma))) * b
        states[2 * i][...] = b_slope
        states[2 * i + 1][...] = act
        term = dot((b_slope * da + act * db).astype(jnp.bfloat16), down_w[0])
        add_term(total, earlier, term)
        earlier = total
    if finish:
        store_parts(total, outs)


def backward_kernel(experts, blocks, start, finish, where_ref, *refs):
    refs = list(refs)
    parts, refs = refs[:6], refs[6:]
    earlier = None if start else refs.pop(0)
    states, refs = refs[: 2 * len(experts)], refs[2 * len(experts) :]
    weights, refs = refs[: 3 * len(experts)], refs[3 * len(experts) :]
    sems, jv, total = refs[-3:]
    outs = refs[:-3]
    squares = outs.pop() if start else None
    if not finish:
        total = outs[0]
    rows = parts[0].shape[0]
    here = pl.ds(blocks[0] * rows, len(blocks) * rows)
    fetch(where_ref[0] == 1, parts, blocks, jv, sems)
    if start:
        sums = jnp.zeros((1, LANES), jnp.float32)
        for column in range(0, jv.shape[1], LANES):
            piece = jv[:, pl.ds(column, LANES)].astype(jnp.float32)
            sums = sums + jnp.sum(piece * piece, axis=0, keepdims=True)
        squares[...] = jnp.broadcast_to(sums, squares.shape)
    for i in range(len(experts)):
        gate_w, up_w, down_w = weights[3 * i : 3 * i + 3]
        back = dot_last(jv[...], down_w[0])
        grad_gate = (back * states[2 * i][here, :]).astype(jnp.bfloat16)
        grad_up = (back * states[2 * i + 1][here, :]).astype(jnp.bfloat16)
        term = dot_last(grad_gate, gate_w[0]) + dot_last(grad_up, up_w[0])
        add_term(total, earlier, term)
        earlier = total
    if finish:
        store_parts(total, outs)


def kernel_call(kernel, name, where, parts, operands, outs, blocks, width, flops):
    anywhere, vmem = pl.BlockSpec(memory_space=pl.ANY), pl.BlockSpec(memory_space=pltpu.VMEM)
    rows = parts[0].shape[0] * blocks
    return pl.pallas_call(
        kernel,
        in_specs=[pl.BlockSpec(memory_space=pltpu.SMEM)]
        + [anywhere] * len(parts)
        + [vmem] * len(operands),
        out_specs=[vmem] * len(outs),
        out_shape=[pltpu.VMEM(shape, kind) for shape, kind in outs],
        scratch_shapes=[
            pltpu.SemaphoreType.DMA((blocks,)),
            pltpu.VMEM((rows, parts[0].shape[1]), jnp.bfloat16),
            pltpu.VMEM((rows, width), jnp.float32),
        ],
        compiler_params=pltpu.CompilerParams(vmem_limit_bytes=10 * 2**20),
        cost_estimate=pl.CostEstimate(flops=flops, bytes_accessed=0, transcendentals=0),
        name=name,
    )(where, *parts, *[in_vmem(value) for value in operands])


def output_kernel(elements, where_ref, squares, whole_a, jv_b, own, side, inner_last, out):
    scale = lax.rsqrt(jnp.sum(squares[pl.ds(0, 1), :], axis=1, keepdims=True) / elements + 1e-06)
    half = whole_a.shape[0]
    out[pl.ds(0, half), :] = whole_a[...] * scale
    total = jv_b[...] + own[...] + side[...].astype(jnp.float32)
    inner = where_ref[0] == 1

    @pl.when(inner)
    def _():
        out[pl.ds(half, half), :] = (total + inner_last[...].astype(jnp.float32)) * scale

    @pl.when(jnp.logical_not(inner))
    def _():
        out[pl.ds(half, half), :] = total * scale


def load_kernel(count, *refs):
    arrays, outs, sems = refs[:count], refs[count : 2 * count], refs[2 * count]
    copies = [
        pltpu.make_async_copy(array, out, sems.at[i]) for i, (array, out) in enumerate(zip(arrays, outs))
    ]
    for copy in copies:
        copy.start()
    for copy in copies:
        copy.wait()


def load(arrays):
    return pl.pallas_call(
        functools.partial(load_kernel, len(arrays)),
        in_specs=[pl.BlockSpec(memory_space=pl.ANY)] * len(arrays),
        out_specs=[pl.BlockSpec(memory_space=pltpu.VMEM)] * len(arrays),
        out_shape=[pltpu.VMEM(array.shape, array.dtype) for array in arrays],
        scratch_shapes=[pltpu.SemaphoreType.DMA((len(arrays),))],
        compiler_params=pltpu.CompilerParams(vmem_limit_bytes=2**20),
        name="load",
    )(*arrays)


def exchange_sum(value, axis, step):
    pairs = [(i, i ^ step) for i in range(lax.axis_size(axis))]
    return value + lax.ppermute(value, axis, pairs)


def gate_pieces(routes, gates, owners):
    rest = jnp.sum(
        jnp.where(
            routes[:, :, None] == jnp.arange(owners, dtype=jnp.int32)[None, None, :],
            gates[:, :, None],
            jnp.float32(0.0),
        ),
        axis=1,
    )
    pieces = []
    for _ in range(GATE_PIECES):
        piece = lax.reduce_precision(rest, 8, 7)
        pieces.append(piece.astype(jnp.bfloat16))
        rest = rest - piece
    return jnp.pad(jnp.concatenate(pieces, axis=1), ((0, 0), (0, LANES - GATE_PIECES * owners)))


def line_shards(tokens, tangent, routes, gates, w_gate, w_up, w_down):
    token_count, width = tokens.shape
    hidden = w_gate.shape[2]
    owners = lax.axis_size("expert")
    me = lax.axis_index("expert")
    pos = me // CORES
    inner = (pos == 1) | (pos == 2)
    where = jnp.stack([inner.astype(jnp.int32), me, me ^ 1])
    half = token_count // 2
    line_rows = LINE * half
    swap = [(i, i ^ 1) for i in range(owners)]

    def pick(ends, inners):
        return jnp.where(inner, inners, ends)

    def home(parts, side, inner_last):
        return parts[0] + side.astype(jnp.float32) + pick(0.0, inner_last.astype(jnp.float32))

    def part_outs(blocks):
        return [((half, width), jnp.float32 if block == 0 else jnp.bfloat16) for block in blocks]

    def forward(parts, experts, earlier=None):
        finish = experts[-1] == CORES - 1
        outs = part_outs(range(LINE)) if finish else [((line_rows, width), jnp.float32)]
        result = kernel_call(
            functools.partial(forward_kernel, owners, experts, experts[0] == 0, finish),
            "forward",
            where,
            parts,
            ([] if earlier is None else [earlier]) + [w for e in experts for w in weights[e]],
            outs + [((line_rows, hidden), jnp.float32)] * (2 * len(experts)),
            LINE,
            width,
            2 * 5 * line_rows * width * hidden * len(experts),
        )
        states = result[len(outs) :]
        return (result[: len(outs)] if finish else result[0]), states

    def backward(parts, states, experts, blocks=tuple(range(LINE)), earlier=None):
        start, finish = experts[0] == 0, experts[-1] == CORES - 1
        rows = len(blocks) * half
        outs = part_outs(blocks) if finish else [((rows, width), jnp.float32)]
        result = kernel_call(
            functools.partial(backward_kernel, experts, blocks, start, finish),
            "backward",
            where,
            parts,
            ([] if earlier is None else [earlier])
            + [s for e in experts for s in states[2 * e : 2 * e + 2]]
            + [w for e in experts for w in weights[e]],
            outs + ([((8, LANES), jnp.float32)] if start else []),
            len(blocks),
            width,
            2 * 3 * rows * width * hidden * len(experts),
        )
        squares = result[-1] if start else None
        return (result[: len(outs)] if finish else result[0]), squares

    pieces = gate_pieces(routes, gates, owners)
    halves = [slice(0, half), slice(half, token_count)]
    load_a, load_b = (
        jnp.concatenate([tokens[rows], tangent[rows], pieces[rows]], axis=1) for rows in halves
    )

    def slot(*results):
        return lax.optimization_barrier(results)

    def both_ways(part, payload):
        first = pick(part, payload[:, :width])
        if payload.shape[1] > width:
            first = jnp.concatenate([first, payload[:, width:]], axis=1)
        return side_hop(first)

    sib = [lax.ppermute(w, "expert", swap) for w in (w_gate, w_up, w_down)]
    a_near, a_side, own_weights, load_b = slot(
        inner_hop(load_a), side_hop(load_a), load((w_gate, w_up, w_down)), load_b
    )
    a_near_end, a_far, sib, first_parts, load_b = slot(
        side_hop(a_near), inner_hop(a_side), sib, load((load_a, a_side, a_near)), load_b
    )
    a_far_end, sib_weights, more_parts, load_b = slot(
        side_hop(a_far), load(sib), load((a_near_end, a_far)), load_b
    )
    a_parts = (*first_parts, *more_parts)
    weights = (own_weights, sib_weights)

    everyone = tuple(range(CORES))
    b_near, b_side, (pa, states_a) = slot(
        inner_hop(load_b),
        side_hop(load_b),
        forward((*a_parts, a_far_end), everyone),
    )
    b_far, b_near_end = (inner_hop(b_side), both_ways(pa[3], b_near))
    sa_far = add_rows(pa[3], b_near_end[:, :width])
    sa_side, b_far_end = slot(inner_hop(sa_far), both_ways(pa[2], b_far))
    sa_near = add_rows(pa[2], b_far_end[:, :width])
    b_parts = (load_b, b_side, b_near, b_near_end, b_far, b_far_end)
    last, came, (sum_b, states_b) = slot(
        inner_hop(sa_near), both_ways(pa[1], add_rows(pa[1], sa_side)), forward(b_parts, everyone[:1])
    )
    jv_a = tangent[:half].astype(jnp.float32) + home(pa, came, last)

    ja = jv_a.astype(jnp.bfloat16)
    near, side, (pb, rest_b) = slot(
        inner_hop(ja), side_hop(ja), forward(b_parts, everyone[1:], sum_b)
    )
    states_b = [*states_b, *rest_b]
    far, near_end = slot(inner_hop(side), both_ways(pb[3], near))
    s_far = add_rows(pb[3], near_end)
    s_side, far_end = (inner_hop(s_far), both_ways(pb[2], far))
    s_near = add_rows(pb[2], far_end)
    ja_parts = (ja, side, near, near_end, far, far_end)
    last, came, (sum_a, squares_a) = slot(
        inner_hop(s_near),
        both_ways(pb[1], add_rows(pb[1], s_side)),
        backward(ja_parts, states_a, everyone[:1]),
    )
    jv_b = tangent[half:].astype(jnp.float32) + home(pb, came, last)

    jb = jv_b.astype(jnp.bfloat16)
    near, side, (ga, _) = slot(
        inner_hop(jb), side_hop(jb), backward(ja_parts, states_a, everyone[1:], earlier=sum_a)
    )
    far, near_end = slot(inner_hop(side), both_ways(ga[3], near))
    s_far = add_rows(ga[3], near_end)
    s_side, far_end = (inner_hop(s_far), both_ways(ga[2], far))
    s_near = add_rows(ga[2], far_end)
    jb_parts = (jb, side, near, near_end, far, far_end)
    last, came, (gb, squares_b) = slot(
        inner_hop(s_near),
        both_ways(ga[1], add_rows(ga[1], s_side)),
        backward(jb_parts, states_b, everyone),
    )
    whole_a = jv_a + home(ga, came, last)

    lines = lax.axis_size("dp")
    squares = exchange_sum(squares_a + squares_b, "expert", 1)
    step = 1
    while step < lines // 2:
        squares = exchange_sum(squares, "dp", step)
        step *= 2
    came, squares = slot(side_hop(gb[3]), squares)
    s_side, came = slot(inner_hop(add_rows(gb[3], came)), side_hop(gb[2]))
    s_near = add_rows(gb[2], came)
    while step < lines:
        squares = exchange_sum(squares, "dp", step)
        step *= 2
    last, came = slot(inner_hop(s_near), side_hop(pick(gb[1], add_rows(gb[1], s_side))))
    vmem = pl.BlockSpec(memory_space=pltpu.VMEM)
    return pl.pallas_call(
        functools.partial(output_kernel, token_count * width * lines * owners),
        in_specs=[pl.BlockSpec(memory_space=pltpu.SMEM)] + [vmem] * 6,
        out_specs=vmem,
        out_shape=jax.ShapeDtypeStruct((token_count, width), jnp.float32),
        compiler_params=pltpu.CompilerParams(vmem_limit_bytes=8 * 2**20),
        name="output",
    )(where, *[in_vmem(value) for value in (squares, whole_a, jv_b, gb[0], came, last)])


def owner_states(x_rows, gate_w, up_w):
    pre_a = dot(x_rows, gate_w)
    pre_b = dot(x_rows, up_w)
    sigma = jax.nn.sigmoid(pre_a)
    act = pre_a * sigma
    slope = sigma * (1.0 + pre_a * (1.0 - sigma))
    return (pre_b, act, slope)


def pair_shards(tokens, tangent, routes, gates, w_gate, w_up, w_down):
    token_count, model_width = tokens.shape
    top_k = routes.shape[1]
    owners = lax.axis_size("expert")
    expert_total = owners * w_gate.shape[0]
    capacity = pair_capacity(token_count, top_k, expert_total)
    slot_total = expert_total * capacity
    pair_count = token_count * top_k
    gate_w = w_gate[0]
    up_w = w_up[0]
    down_w = w_down[0]
    flat_routes = routes.reshape(pair_count)
    onehot = (flat_routes[:, None] == jnp.arange(expert_total, dtype=jnp.int32)[None, :]).astype(
        jnp.int32
    )
    before = jnp.cumsum(onehot, axis=0) - onehot
    slot_of = jnp.sum(before * onehot, axis=1)
    slot_index = flat_routes * capacity + slot_of
    slot_match = slot_index[None, :] == jnp.arange(slot_total, dtype=jnp.int32)[:, None]
    filled = jnp.any(slot_match, axis=1)
    pair_token = jnp.arange(pair_count, dtype=jnp.int32) // top_k
    source_token = jnp.sum(jnp.where(slot_match, pair_token[None, :], 0), axis=1)
    source_gate = jnp.sum(
        jnp.where(slot_match, gates.reshape(pair_count)[None, :], jnp.float32(0.0)), axis=1
    )
    keep_mask = filled.astype(jnp.bfloat16)[:, None]

    def exchange(rows):
        blocks = rows.reshape(owners, capacity, model_width)
        moved = lax.all_to_all(blocks, "expert", split_axis=0, concat_axis=0, tiled=True)
        return moved.reshape(slot_total, model_width)

    x_rows = exchange(jnp.take(tokens, source_token, axis=0) * keep_mask)
    v_rows = exchange(jnp.take(tangent, source_token, axis=0) * keep_mask)
    pre_b, act, slope = owner_states(x_rows, gate_w, up_w)
    tan_a = dot(v_rows, gate_w)
    tan_b = dot(v_rows, up_w)
    hidden_tangent = (slope * tan_a * pre_b + act * tan_b).astype(jnp.bfloat16)
    returned = exchange(dot(hidden_tangent, down_w).astype(jnp.bfloat16))
    picked_rows = jnp.take(returned, slot_index, axis=0)
    picked_rows = picked_rows.reshape(token_count, top_k, model_width)
    jv_vals = tangent.astype(jnp.float32) + jnp.sum(
        gates[:, :, None] * picked_rows.astype(jnp.float32), axis=1
    )
    cot_rows = exchange(
        (jnp.take(jv_vals, source_token, axis=0) * source_gate[:, None]).astype(jnp.bfloat16)
    )
    back_vals = dot_last(cot_rows, down_w)
    grad_gate = (back_vals * pre_b * slope).astype(jnp.bfloat16)
    grad_up = (back_vals * act).astype(jnp.bfloat16)
    pair_grad = dot_last(grad_gate, gate_w) + dot_last(grad_up, up_w)
    grad_rows = jnp.take(exchange(pair_grad.astype(jnp.bfloat16)), slot_index, axis=0)
    grad_rows = grad_rows.reshape(token_count, top_k, model_width)
    summed = jv_vals + jnp.sum(grad_rows.astype(jnp.float32), axis=1)
    global_sum = lax.psum(jnp.sum(jv_vals * jv_vals), ("dp", "expert"))
    element_count = token_count * lax.axis_size("dp") * owners * model_width
    return summed * lax.rsqrt(global_sum / element_count + 1e-06)


def pair_capacity(token_count, top_k, expert_total):
    return max(2, token_count * top_k * 9 // (8 * expert_total))


def shards(tokens, tangent, routes, gates, w_gate, w_up, w_down):
    token_count, top_k = routes.shape
    owners = lax.axis_size("expert")
    capacity = pair_capacity(token_count, top_k, owners * w_gate.shape[0])
    dp = lax.axis_size("dp")
    whole_blocks = (
        owners == CORES * LINE
        and dp & (dp - 1) == 0
        and w_gate.shape[0] == 1
        and token_count <= CORES * capacity
    )
    form = line_shards if whole_blocks else pair_shards
    return form(tokens, tangent, routes, gates, w_gate, w_up, w_down)


def solution(mesh):
    placed = (
        P(("dp", "expert"), None),
        P(("dp", "expert"), None),
        P(("dp", "expert"), None),
        P(("dp", "expert"), None),
        P("expert", None, None),
        P("expert", None, None),
        P("expert", None, None),
    )
    return jax.shard_map(
        shards, mesh=mesh, in_specs=placed, out_specs=P(("dp", "expert"), None), check_vma=False
    )
```
